128 devices in a mesh: seq: 32 (over z, y, core), fsdp: 4 (over x).
Axes of the slice: x: 4, y: 4, z: 4, core: 2. Of those that a mesh axis runs over, the one named last changes fastest.
Arguments:
- self_query: bfloat16 [4, 8192, 2048], P('fsdp', 'seq'), may hold values from -8 to 8, as said below
- self_key: bfloat16 [4, 8192, 2048], P('fsdp', 'seq'), may hold values from -8 to 8, as said below
- self_value: bfloat16 [4, 8192, 2048], P('fsdp', 'seq'), may hold values from -6 to 6
- cross_query: bfloat16 [4, 8192, 2048], P('fsdp', 'seq'), may hold values from -6 to 6
- neighbours: bfloat16 [4, 128, 256, 768], P('fsdp', 'seq'), may hold values from -6 to 6
- neighbour_count: int32 [4, 128], P('fsdp', 'seq'), may hold values from 1 to 2
- kv_weight: bfloat16 [768, 4096], P('fsdp'), may hold values from -0.21875 to 0.21875
- out_grad: bfloat16 [4, 8192, 2048], P('fsdp', 'seq'), may hold values from -6 to 6
Outputs:
- block_out: bfloat16 [4, 8192, 2048], P('fsdp', 'seq')
- query_grad: bfloat16 [4, 8192, 2048], P('fsdp', 'seq')
- key_grad: bfloat16 [4, 8192, 2048], P('fsdp', 'seq')
- value_grad: bfloat16 [4, 8192, 2048], P('fsdp', 'seq')
- cross_grad: bfloat16 [4, 8192, 2048], P('fsdp', 'seq')
- weight_grad: float32 [768, 4096], P(('seq', 'fsdp'))
The draws below stay inside these ranges and needn't reach their ends.
Inputs may be any that keep to these rules, and one draw needn't show every extreme that they name: `self_query`: entries of order one. `self_key`: entries of order one.
All inputs are finite; a program needn't handle non-finite values.
Results may differ from the reference program's by a relative error of at most 0.014.
Values may be sent and summed in bfloat16 or wider, within the bound.
A program may use at most 192 MiB of HBM per device.

```python
import jax
import jax.numpy as jnp
from jax import lax

HEADS = 16
HD = 128
ENC = 768
GROUP = 64
NEIGH = 2
RLEN = 128
HW = 2048
NB = 256
WINDOW = 256
FILES = 4
SEQ_LEN = 8192
GROUPS = 128


def draw_self_query(key, part):
    values_drawn = jnp.clip(jax.random.normal(jax.random.fold_in(key, 1), (FILES, SEQ_LEN, HW), jnp.float32), -6.0, 6.0)
    return values_drawn.astype(jnp.bfloat16)


def draw_self_key(key, part):
    values_drawn = jnp.clip(jax.random.normal(jax.random.fold_in(key, 2), (FILES, SEQ_LEN, HW), jnp.float32), -6.0, 6.0)
    return values_drawn.astype(jnp.bfloat16)


def set_ends(values, own_key, least, high):
    longest = values.shape.index(max(values.shape))
    spots = []
    for shift in (0, 1):
        where = [jax.random.randint(jax.random.fold_in(own_key, axis), (), 0, length) for axis, length in enumerate(values.shape)]
        where[longest] = (where[longest] + shift) % values.shape[longest]
        spots.append(tuple(where))
    return values.at[spots[0]].set(least).at[spots[1]].set(high)


def with_spikes(entries, stream_key, source, target, shards_of, factor):
    def block_of(dim):
        return (jnp.arange(entries.shape[dim]) // (entries.shape[dim] // shards_of)).reshape((-1,) + (1,) * (entries.ndim - 1 - dim))

    one_side = jax.random.permutation(stream_key, shards_of)[block_of(target)]
    second = (block_of(target) + shards_of // 2) % shards_of
    return jnp.where((block_of(source) == one_side) | (block_of(source) == second), factor * entries, entries)


def levels(rng, shape, pieces, least, top_value):
    factor_of, own = 1.0, jax.random.fold_in(rng, 6)
    for axis_at, parts in pieces:
        draws = jnp.exp(jax.random.uniform(jax.random.fold_in(own, axis_at), (parts,), jnp.float32, least / len(pieces), top_value / len(pieces)))
        factor_of = factor_of * jnp.repeat(draws, shape[axis_at] // parts).reshape([-1 if axis == axis_at else 1 for axis in range(len(shape))])
    return factor_of


def centred(key, dims, deviation, most, cuts=(), kind=jnp.bfloat16):
    gain = levels(key, dims, cuts, -0.22, 0.18) if cuts else 1.0
    drawn = jax.random.normal(key, dims, jnp.float32) * deviation * gain
    return jnp.minimum(jnp.maximum(drawn, -most), most).astype(kind)


def gaussian_with(rng, extent, width, most, pieces, heavy, kind=jnp.bfloat16):
    entries = width * jax.random.normal(rng, extent, jnp.float32)
    if pieces:
        entries = entries * levels(rng, extent, pieces, -0.22, 0.18)
    return jnp.clip(with_spikes(entries, jax.random.fold_in(rng, 3), *heavy), -most, most).astype(kind)


def setup_inputs(seed: int = 0) -> dict:
    seeds = jax.random.split(jax.random.key(seed), 9)
    self_query = draw_self_query(jax.random.fold_in(seeds[8], 71), 0)
    self_key = draw_self_key(jax.random.fold_in(seeds[8], 71), 0)
    self_value = centred(seeds[2], (FILES, SEQ_LEN, HW), 1.0, 6.0, ((0, 4), (1, 32)))
    cross_query = centred(seeds[3], (FILES, SEQ_LEN, HW), 1.0, 6.0, ((0, 4), (1, 32)))
    neighbours = gaussian_with(seeds[4], (FILES, GROUPS, NB, ENC), 1.0, 6.0, ((0, 4), (1, 32)), (1, 3, 32, 2.75))
    neighbour_count = set_ends(jax.random.randint(seeds[5], (FILES, GROUPS), 1, NEIGH + 1), jax.random.fold_in(seeds[5], 1), 1, NEIGH).astype(jnp.int32)
    kv_weight = centred(seeds[6], (ENC, 2 * HW), ENC ** -0.5, 0.21875, ((0, 4),))
    out_grad = centred(seeds[7], (FILES, SEQ_LEN, HW), 1.0, 6.0, ((0, 4), (1, 32)))
    return {"self_query": self_query, "self_key": self_key, "self_value": self_value, "cross_query": cross_query, "neighbours": neighbours, "neighbour_count": neighbour_count, "kv_weight": kv_weight, "out_grad": out_grad}


neg_fill = -1e30


def attend(queries, keys_in, values_in, grads, allowed, scaling):
    query_full = queries.astype(jnp.float32)
    key_full = keys_in.astype(jnp.float32)
    value_full = values_in.astype(jnp.float32)
    grad_full = grads.astype(jnp.float32)
    scores = jnp.einsum("...qhd,...khd->...hqk", query_full, key_full) * scaling
    scores = jnp.where(allowed, scores, neg_fill)
    peaks = jnp.max(scores, axis=-1, keepdims=True)
    weights = jnp.exp(scores - peaks)
    probs = weights / jnp.sum(weights, axis=-1, keepdims=True)
    probs_low = lax.optimization_barrier(probs.astype(jnp.bfloat16)).astype(jnp.float32)
    output = jnp.einsum("...hqk,...khd->...qhd", probs_low, value_full)
    prob_grad = jnp.einsum("...qhd,...khd->...hqk", grad_full, value_full)
    row_delta = jnp.sum(probs * prob_grad, axis=-1, keepdims=True)
    score_grad = lax.optimization_barrier((probs * (prob_grad - row_delta) * scaling).astype(jnp.bfloat16)).astype(jnp.float32)
    query_grad = jnp.einsum("...hqk,...khd->...qhd", score_grad, key_full)
    key_grad = jnp.einsum("...hqk,...qhd->...khd", score_grad, query_full)
    value_grad = jnp.einsum("...hqk,...qhd->...khd", probs_low, grad_full)
    return output, query_grad, key_grad, value_grad


def self_file(query_file, key_file, value_file, grad_file):
    tok_rows = WINDOW
    blocks = SEQ_LEN // tok_rows
    scaling = HD ** -0.5

    def blocked(array):
        return array.reshape(blocks, tok_rows, HEADS, HD)

    zero_block = jnp.zeros((1, tok_rows, HEADS, HD), jnp.bfloat16)
    key_blocks = blocked(key_file)
    value_blocks = blocked(value_file)
    key_before = jnp.concatenate([zero_block, key_blocks[:-1]], 0)
    value_before = jnp.concatenate([zero_block, value_blocks[:-1]], 0)
    row_index = jnp.arange(tok_rows, dtype=jnp.int32)[:, None]
    col_index = jnp.arange(2 * tok_rows, dtype=jnp.int32)[None, :]

    def one_block(inputs):
        query_block, key_prev, key_own, value_prev, value_own, grad_block, block_id = inputs
        allowed = (col_index > row_index) & (col_index <= row_index + tok_rows) & ((col_index >= tok_rows) | (block_id > 0))
        return attend(query_block, jnp.concatenate([key_prev, key_own], 0), jnp.concatenate([value_prev, value_own], 0), grad_block, allowed[None], scaling)

    output, query_grad, key_terms, value_terms = lax.map(one_block, (blocked(query_file), key_before, key_blocks, value_before, value_blocks, blocked(grad_file), jnp.arange(blocks, dtype=jnp.int32)))
    zero_terms = jnp.zeros((1, tok_rows, HEADS, HD), jnp.float32)
    key_grad = key_terms[:, tok_rows:] + jnp.concatenate([key_terms[1:, :tok_rows], zero_terms], 0)
    value_grad = value_terms[:, tok_rows:] + jnp.concatenate([value_terms[1:, :tok_rows], zero_terms], 0)
    return output.reshape(SEQ_LEN, HW), query_grad.reshape(SEQ_LEN, HW), key_grad.reshape(SEQ_LEN, HW), value_grad.reshape(SEQ_LEN, HW)


def cross_file(query_file, grad_file, neigh_file, count_file, kv_weight):
    neigh_rows = NEIGH * RLEN
    scaling = HD ** -0.5
    flat_neigh = neigh_file.reshape(GROUPS * neigh_rows, ENC)
    kv_proj = jnp.dot(flat_neigh, kv_weight, preferred_element_type=jnp.float32).astype(jnp.bfloat16).reshape(GROUPS, neigh_rows, 2 * HW)
    keys_all = kv_proj[..., :HW].reshape(GROUPS, neigh_rows, HEADS, HD)
    values_all = kv_proj[..., HW:].reshape(GROUPS, neigh_rows, HEADS, HD)
    key_before = jnp.concatenate([keys_all[:1], keys_all[:-1]], 0)
    value_before = jnp.concatenate([values_all[:1], values_all[:-1]], 0)
    count_before = jnp.concatenate([count_file[:1], count_file[:-1]], 0)
    neighbour_of = jnp.arange(neigh_rows, dtype=jnp.int32) // RLEN

    def one_group(inputs):
        query_group, grad_group, key_group, value_group, count_group, group_id = inputs
        allowed = (neighbour_of < count_group)[None, None, :]
        output, query_grad, key_grad, value_grad = attend(query_group, key_group, value_group, grad_group, allowed, scaling)
        live = group_id > 0
        output = jnp.where(live, output, 0.0)
        query_grad = jnp.where(live, query_grad, 0.0)
        kv_grad = jnp.concatenate([key_grad.reshape(neigh_rows, HW), value_grad.reshape(neigh_rows, HW)], -1)
        kv_grad = jnp.where(live, kv_grad, 0.0).astype(jnp.bfloat16)
        return output, query_grad, kv_grad

    group_view = (GROUPS, GROUP, HEADS, HD)
    output, query_grad, kv_grads = lax.map(one_group, (query_file.reshape(group_view), grad_file.reshape(group_view), key_before, value_before, count_before, jnp.arange(GROUPS, dtype=jnp.int32)))
    kv_grad_group = jnp.concatenate([kv_grads[1:], jnp.zeros((1, neigh_rows, 2 * HW), jnp.bfloat16)], 0)
    weight_part = jnp.dot(flat_neigh.T, kv_grad_group.reshape(GROUPS * neigh_rows, 2 * HW), preferred_element_type=jnp.float32)
    return output.reshape(SEQ_LEN, HW), query_grad.reshape(SEQ_LEN, HW), weight_part


def reference(self_query, self_key, self_value, cross_query, neighbours, neighbour_count, kv_weight, out_grad):
    def one_file(inputs):
        query_file, key_file, value_file, cross_file_q, neigh_file, count_file, grad_file = inputs
        self_out, query_grad, key_grad, value_grad = self_file(query_file, key_file, value_file, grad_file)
        cross_out, cross_grad, weight_part = cross_file(cross_file_q, grad_file, neigh_file, count_file, kv_weight)
        block_out = (self_out + cross_out).astype(jnp.bfloat16)
        return block_out, query_grad.astype(jnp.bfloat16), key_grad.astype(jnp.bfloat16), value_grad.astype(jnp.bfloat16), cross_grad.astype(jnp.bfloat16), weight_part

    block_out, query_grad, key_grad, value_grad, cross_grad, weight_parts = lax.map(one_file, (self_query, self_key, self_value, cross_query, neighbours, neighbour_count, out_grad))
    weight_grad = jnp.sum(weight_parts, axis=0)
    return (block_out, query_grad, key_grad, value_grad, cross_grad, weight_grad)
```

```python
import jax
import jax.numpy as jnp
import numpy as np
from jax import lax
from jax.experimental import pallas as pl
from jax.experimental.pallas import tpu as pltpu
from jax.sharding import PartitionSpec as P

HEADS = 16
HD = 128
GROUP = 64
RLEN = 128
ENC = 768
TOK = 256
PAIRS = 8
PW = 256
SLABS = 32
SCALE = HD**-0.5
MESH_ID = pl.DeviceIdType.MESH
F32 = jnp.float32
BF16 = jnp.bfloat16

NN = (((1,), (0,)), ((), ()))
NT = (((1,), (1,)), ((), ()))
TN = (((0,), (0,)), ((), ()))


def dot(a, b, dims=NN):
    return lax.dot_general(a, b, dims, preferred_element_type=F32)


def row_orders():
    sizes = {"z": 4, "y": 4, "c": 2, "x": 4}
    grids = np.meshgrid(*[np.arange(n) for n in (2, 4, 4, 4, 6)], indexing="ij")
    out = np.zeros((3, ENC, ENC), np.float32)
    for t, axes in enumerate(("xyz", "yzx", "zxy")):
        at = {"c": grids[0], axes[0]: grids[1], axes[1]: grids[2], axes[2]: grids[3]}
        natural = (((at["z"] * sizes["y"] + at["y"]) * 2 + at["c"]) * 4 + at["x"]) * 6 + grids[4]
        out[t, np.arange(ENC), natural.reshape(-1)] = 1.0
    return out.astype(BF16)


def mod(a, n):
    return lax.rem(a, n)


def kernel(
    q_h, k_h, v_h, cq_h, nb_h, cnt_s, w_h, do_h, pt_h,
    out_o, dq_o, dk_o, dv_o, dcq_o, dw_o,
    qv, cqv, dov, kv, nbx, ptv, nbt, wv, kvret, kvsend, kvown, stage,
    bias, selfout, dkv, cntv, cntsend,
    own, csend, crecv, own1, t1, s1send, s1recv, own2, s2send, s2recv, t2, s3buf, s3recv,
    load_sem, pt_sem, tok_sem, nb_sem, nbh_sem, cnt_sem, kvx_sem, w_sem, ret_sem, out_sem, rs_sem,
):
    s = lax.axis_index("seq")
    x = lax.axis_index("fsdp")
    c = mod(s, 2)
    y = mod(s // 2, 4)
    z = s // 8
    first = s == 0
    nxt = mod(s + 1, SLABS)
    prv = mod(s + SLABS - 1, SLABS)
    sib = s + 1 - 2 * c
    xr = mod(x + 1, 4)
    xl = mod(x + 3, 4)
    xa = mod(x + 2, 4)

    def seq_of(zz, yy):
        return (zz * 4 + yy) * 2 + c

    def dev(seq, fs):
        return {"seq": seq, "fsdp": fs}

    def remote(src, dst, ssem, rsem, where):
        return pltpu.make_async_remote_copy(
            src_ref=src, dst_ref=dst, send_sem=ssem, recv_sem=rsem, device_id=where, device_id_type=MESH_ID
        )

    def wait(ref, sem):
        pltpu.make_async_copy(ref, ref, sem).wait()

    def rows(start, size):
        return pl.ds(pl.multiple_of(start, 8), size)

    def cols(start, size):
        return pl.ds(pl.multiple_of(start, 128), size)

    def load_w(p, _):
        for half in range(2):
            pltpu.make_async_copy(
                w_h.at[:, cols(half * 2048 + p * PW, PW)],
                wv.at[p, rows(x * 192, 192), pl.ds(half * PW, PW)],
                load_sem.at[p],
            ).start()
        return 0

    lax.fori_loop(0, PAIRS, load_w, 0)
    own_nb = pltpu.make_async_copy(nb_h.at[pl.ds(0, 768)], nbx.at[pl.ds(256, 768)], nb_sem)
    own_nb.start()
    pt_copy = pltpu.make_async_copy(pt_h, ptv, pt_sem)
    pt_copy.start()

    def load_tokens(p, _):
        span = cols(p * PW, PW)
        for n, (src, dst) in enumerate(
            ((q_h, qv.at[p]), (do_h, dov.at[p]), (cq_h, cqv.at[p]), (k_h, kv.at[p, 0, pl.ds(256, 256)]), (v_h, kv.at[p, 1, pl.ds(256, 256)]))
        ):
            pltpu.make_async_copy(src.at[:, span], dst, tok_sem.at[p, n]).start()
        return 0

    lax.fori_loop(0, PAIRS, load_tokens, 0)

    for g in range(3):
        cntv[g + 1] = jnp.full((8, 128), cnt_s[0, g], jnp.int32)
    cntsend[...] = jnp.full((8, 128), cnt_s[0, 3], jnp.int32)
    s3buf[...] = jnp.zeros(s3buf.shape, F32)

    barrier = pltpu.get_barrier_semaphore()
    partners = [dev(sib, x), dev(nxt, x), dev(prv, x)]
    for d in range(1, 4):
        partners += [dev(s, mod(x + d, 4)), dev(seq_of(z, mod(y + d, 4)), x), dev(seq_of(mod(z + d, 4), y), x)]
    for partner in partners:
        pl.semaphore_signal(barrier, inc=1, device_id=partner, device_id_type=MESH_ID)
    pl.semaphore_wait(barrier, len(partners))

    def w_first(p):
        wait(wv.at[p, rows(x * 192, 192)], load_sem.at[p])
        piece = wv.at[p, rows(x * 192 + c * 96, 96)]
        for where in (xr, xl):
            remote(piece, piece, w_sem.at[0, p], w_sem.at[1, p], dev(s, where)).start()

    def w_second(p):
        wait(wv.at[p, pl.ds(0, 192)], w_sem.at[1, p])
        from_left = wv.at[p, rows(xl * 192 + c * 96, 48)]
        from_right = wv.at[p, rows(xr * 192 + c * 96 + 48, 48)]
        remote(from_left, from_left, w_sem.at[2, p], w_sem.at[3, p], dev(s, xr)).start()
        remote(from_right, from_right, w_sem.at[2, p], w_sem.at[3, p], dev(s, xl)).start()
        for shard in (xl, xr):
            piece = wv.at[p, rows(shard * 192 + c * 96, 96)]
            remote(piece, piece, w_sem.at[4, p], w_sem.at[5, p], dev(sib, x)).start()

    def w_third(p):
        wait(wv.at[p, pl.ds(0, 96)], w_sem.at[3, p])
        piece = wv.at[p, rows(xa * 192 + c * 96, 96)]
        remote(piece, piece, w_sem.at[4, p], w_sem.at[5, p], dev(sib, x)).start()

    def w_done(p):
        wait(wv.at[p, pl.ds(0, 288)], w_sem.at[5, p])

    w_first(0)
    halo = remote(nb_h.at[pl.ds(768, 256)], nbx.at[pl.ds(0, 256)], nbh_sem.at[0], nbh_sem.at[1], dev(nxt, x))
    halo.start()
    count_copy = remote(cntsend, cntv.at[0], cnt_sem.at[0], cnt_sem.at[1], dev(nxt, x))
    count_copy.start()

    def send_kv(p, _):
        span = cols(p * PW, PW)
        for n, src in enumerate((k_h, v_h)):
            remote(src.at[:, span], kv.at[p, n, pl.ds(0, 256)], kvx_sem.at[0, p], kvx_sem.at[1, p], dev(nxt, x)).start()
        return 0

    lax.fori_loop(0, PAIRS, send_kv, 0)
    w_first(1)
    w_first(2)

    key_at = lax.broadcasted_iota(jnp.int32, (512, TOK), 0)
    query_at = lax.broadcasted_iota(jnp.int32, (512, TOK), 1)
    allowed = (key_at > query_at) & (key_at <= query_at + TOK) & ((key_at >= TOK) | jnp.logical_not(first))
    bias[...] = jnp.where(allowed, 0.0, -1e30).astype(F32)

    pt_copy.wait()
    own_nb.wait()

    def reorder(n, _):
        t = n // 3
        g = mod(n, 3) + 1
        nbt[t, :, cols(g * 256, 256)] = dot(ptv[t], nbx[rows(g * 256, 256)], NT).astype(BF16)
        return 0

    lax.fori_loop(0, 9, reorder, 0)
    w_second(0)
    w_first(3)
    halo.wait_recv()

    def reorder_halo(t, _):
        nbt[t, :, pl.ds(0, 256)] = dot(ptv[t], nbx[pl.ds(0, 256)], NT).astype(BF16)
        return 0

    lax.fori_loop(0, 3, reorder_halo, 0)
    count_copy.wait_recv()
    w_third(0)
    w_second(1)

    def softmax_grads(sc, dp):
        e = jnp.exp(sc - jnp.max(sc, axis=0, keepdims=True))
        probs = e * (1.0 / jnp.sum(e, axis=0, keepdims=True))
        delta = jnp.sum(probs * dp, axis=0, keepdims=True)
        return probs, probs * (dp - delta) * SCALE

    def self_pair(p):
        for n, ref in enumerate((qv.at[p], dov.at[p], cqv.at[p], kv.at[p, 0, pl.ds(256, 256)], kv.at[p, 1, pl.ds(256, 256)])):
            wait(ref, tok_sem.at[p, n])
        wait(kv.at[p, :, pl.ds(0, 256)], kvx_sem.at[1, p])
        slot = mod(p, 3)
        for h in range(2):
            lanes = pl.ds(h * HD, HD)
            qh = qv[p, :, lanes]
            doh = dov[p, :, lanes]
            kh = kv[p, 0, :, lanes]
            vh = kv[p, 1, :, lanes]
            sc = dot(kh, qh, NT) * SCALE + bias[...]
            probs, ds = softmax_grads(sc, dot(vh, doh, NT))
            probs = probs.astype(BF16)
            ds = ds.astype(BF16)
            selfout[:, lanes] = dot(probs, vh, TN)
            stage[1, p, :, lanes] = dot(ds, kh, TN).astype(BF16)
            dk = dot(ds, qh)
            dv = dot(probs, doh)
            kvsend[p, 0, :, lanes] = dk[:TOK].astype(BF16)
            kvsend[p, 1, :, lanes] = dv[:TOK].astype(BF16)
            kvown[slot, 0, :, lanes] = dk[TOK:]
            kvown[slot, 1, :, lanes] = dv[TOK:]
        remote(kvsend.at[p], kvret.at[p], ret_sem.at[0, p], ret_sem.at[1, p], dev(prv, x)).start()

    def returned(p):
        wait(kvret.at[p], ret_sem.at[1, p])
        slot = mod(p, 3)
        for n, dst in enumerate((dk_o, dv_o)):
            stage[3 + n, p] = (kvown[slot, n] + kvret[p, n].astype(F32)).astype(BF16)
            pltpu.make_async_copy(stage.at[3 + n, p], dst.at[:, cols(p * PW, PW)], out_sem.at[3 + n, p]).start()

    def cross_pair(p):
        lane = lax.broadcasted_iota(jnp.int32, (GROUP, PW), 1)
        key_row = lax.broadcasted_iota(jnp.int32, (256, 128), 0)

        def one_group(g, _):
            tok = rows(g * GROUP, GROUP)
            proj = dot(nbx[rows(g * 256, 256)], wv[p]).astype(BF16)
            kp = proj[:, :PW]
            vp = proj[:, PW:]
            qg = cqv[p, tok, :]
            dog = dov[p, tok, :]
            zero = jnp.zeros((GROUP, PW), BF16)
            qb = jnp.concatenate([jnp.where(lane < HD, qg, zero), jnp.where(lane >= HD, qg, zero)], 0)
            dob = jnp.concatenate([jnp.where(lane < HD, dog, zero), jnp.where(lane >= HD, dog, zero)], 0)
            used = key_row < cntv[g, pl.ds(0, 1), :] * RLEN
            sc = jnp.where(used, dot(kp, qb, NT) * SCALE, -1e30)
            probs, ds = softmax_grads(sc, dot(vp, dob, NT))
            live = jnp.where(jnp.logical_and(first, g == 0), 0.0, 1.0).astype(F32)
            probs = (probs * live).astype(BF16)
            ds = (ds * live).astype(BF16)
            o = dot(probs, vp, TN)
            dq = dot(ds, kp, TN)
            o = jnp.concatenate([o[:GROUP, :HD], o[GROUP:, HD:]], 1)
            dq = jnp.concatenate([dq[:GROUP, :HD], dq[GROUP:, HD:]], 1)
            stage[0, p, tok, :] = (selfout[tok, :] + o).astype(BF16)
            stage[2, p, tok, :] = dq.astype(BF16)
            dkv[rows(g * 256, 256), pl.ds(0, PW)] = dot(ds, qb).astype(BF16)
            dkv[rows(g * 256, 256), pl.ds(PW, PW)] = dot(probs, dob).astype(BF16)
            return 0

        lax.fori_loop(0, 4, one_group, 0)
        for n, dst in enumerate((out_o, dq_o, dcq_o)):
            pltpu.make_async_copy(stage.at[n, p], dst.at[:, cols(p * PW, PW)], out_sem.at[n, p]).start()

    def places(u):
        t = mod(u, 3)
        i0, i1, i2 = (3 - t) // 3, mod(t, 2), t // 2
        return (i0, i1, i2), (i0 * x + i1 * y + i2 * z, i0 * y + i1 * z + i2 * x, i0 * z + i1 * x + i2 * y)

    def peer(u, order, d):
        (i0, i1, i2), _ = places(u)
        on = ((i0, i1, i2), (i2, i0, i1), (i1, i2, i0))[order]
        return dev(seq_of(mod(z + d * on[2], 4), mod(y + d * on[1], 4)), mod(x + d * on[0], 4))

    def weight_grad(p):
        slot = mod(p, 2)
        for n in range(2):
            u = 2 * p + n
            t = mod(u, 3)
            grads = dkv[:, pl.ds(n * PW, PW)]
            csend[u] = dot(nbt[t, rows((1 - c) * 384, 384), :], grads).astype(BF16)
            remote(csend.at[u], crecv.at[u], rs_sem.at[0, u], rs_sem.at[1, u], dev(sib, x)).start()
        for n in range(2):
            u = 2 * p + n
            t = mod(u, 3)
            grads = dkv[:, pl.ds(n * PW, PW)]
            own[slot, n] = dot(nbt[t, rows(c * 384, 384), :], grads)

    def rs_core(p, n):
        u = 2 * p + n
        slot = mod(p, 2)
        _, (m1, _, _) = places(u)
        wait(crecv.at[u], rs_sem.at[1, u])
        for d in (2, 1, 3):
            span = rows(mod(m1 + d, 4) * 96, 96)
            s1send[u, d - 1] = (own[slot, n, span, :] + crecv[u, span, :].astype(F32)).astype(BF16)
            remote(s1send.at[u, d - 1], s1recv.at[u, d - 1], rs_sem.at[2, u], rs_sem.at[3, u], peer(u, 0, d)).start()
        span = rows(m1 * 96, 96)
        own1[slot, n] = own[slot, n, span, :] + crecv[u, span, :].astype(F32)

    def rs_first(p, n):
        u = 2 * p + n
        slot = mod(p, 2)
        _, (_, m2, _) = places(u)
        wait(s1recv.at[u], rs_sem.at[3, u])
        t1[...] = own1[slot, n] + ((s1recv[u, 0].astype(F32) + s1recv[u, 1].astype(F32)) + s1recv[u, 2].astype(F32))
        for d in (2, 1, 3):
            s2send[u, d - 1] = t1[rows(mod(m2 + d, 4) * 24, 24), :]
            remote(s2send.at[u, d - 1], s2recv.at[u, d - 1], rs_sem.at[4, u], rs_sem.at[5, u], peer(u, 1, d)).start()
        own2[slot, n] = t1[rows(m2 * 24, 24), :]

    def rs_second(p, n):
        u = 2 * p + n
        slot = mod(p, 2)
        _, (_, _, m3) = places(u)
        wait(s2recv.at[u], rs_sem.at[5, u])
        total = own2[slot, n] + ((s2recv[u, 0] + s2recv[u, 1]) + s2recv[u, 2])
        for a in range(4):
            s3buf[u, a, pl.ds(0, 6), :] = total[a * 6 : a * 6 + 6]
        for d in (2, 1, 3):
            remote(s3buf.at[u, mod(m3 + d, 4)], s3recv.at[u, d - 1], rs_sem.at[6, u], rs_sem.at[7, u], peer(u, 2, d)).start()

    def rs_third(p, n):
        u = 2 * p + n
        _, (_, _, m3) = places(u)
        wait(s3recv.at[u], rs_sem.at[7, u])
        dw_o[:, cols(n * 2048 + p * PW, PW)] = s3buf[u, m3] + ((s3recv[u, 0] + s3recv[u, 1]) + s3recv[u, 2])

    def step(i, _):
        @pl.when(i < PAIRS - 2)
        def _():
            w_second(i + 2)

        @pl.when(i < PAIRS - 4)
        def _():
            w_first(i + 4)

        @pl.when(i < PAIRS)
        def _():
            self_pair(i)

        @pl.when(i < PAIRS - 1)
        def _():
            w_third(i + 1)

        for lag, stage_of in ((1, rs_core), (2, rs_first), (3, rs_second), (4, rs_third)):

            @pl.when((i >= lag) & (i < PAIRS + lag))
            def _(lag=lag, stage_of=stage_of):
                for n in range(2):
                    stage_of(i - lag, n)

        @pl.when((i >= 2) & (i < PAIRS + 2))
        def _():
            returned(i - 2)

        @pl.when(i < PAIRS)
        def _():
            w_done(i)
            cross_pair(i)
            weight_grad(i)

        return 0

    lax.fori_loop(0, PAIRS + 4, step, 0)

    halo.wait_send()
    count_copy.wait_send()

    def drain(p, _):
        wait(kv.at[p, :, pl.ds(0, 256)], kvx_sem.at[0, p])
        wait(wv.at[p, pl.ds(0, 192)], w_sem.at[0, p])
        wait(wv.at[p, pl.ds(0, 96)], w_sem.at[2, p])
        wait(wv.at[p, pl.ds(0, 288)], w_sem.at[4, p])
        wait(kvsend.at[p], ret_sem.at[0, p])
        for n, dst in enumerate((out_o, dq_o, dcq_o, dk_o, dv_o)):
            pltpu.make_async_copy(stage.at[n, p], dst.at[:, cols(p * PW, PW)], out_sem.at[n, p]).wait()
        for n in range(2):
            u = 2 * p + n
            wait(csend.at[u], rs_sem.at[0, u])
            wait(s1send.at[u], rs_sem.at[2, u])
            wait(s2send.at[u], rs_sem.at[4, u])
            wait(s3recv.at[u], rs_sem.at[6, u])
        return 0

    lax.fori_loop(0, PAIRS, drain, 0)


def on_device(
    self_query, self_key, self_value, cross_query, neighbours, neighbour_count, kv_weight, out_grad
):
    any_spec = pl.BlockSpec(memory_space=pl.ANY)
    slab = jax.ShapeDtypeStruct((TOK, HEADS * HD), BF16)
    dma = pltpu.SemaphoreType.DMA
    subs = 2 * PAIRS
    scratch = [
        pltpu.VMEM((PAIRS, TOK, PW), BF16),
        pltpu.VMEM((PAIRS, TOK, PW), BF16),
        pltpu.VMEM((PAIRS, TOK, PW), BF16),
        pltpu.VMEM((PAIRS, 2, 2 * TOK, PW), BF16),
        pltpu.VMEM((1024, ENC), BF16),
        pltpu.VMEM((3, ENC, ENC), BF16),
        pltpu.VMEM((3, ENC, 1024), BF16),
        pltpu.VMEM((PAIRS, ENC, 2 * PW), BF16),
        pltpu.VMEM((PAIRS, 2, TOK, PW), BF16),
        pltpu.VMEM((PAIRS, 2, TOK, PW), BF16),
        pltpu.VMEM((3, 2, TOK, PW), F32),
        pltpu.VMEM((5, PAIRS, TOK, PW), BF16),
        pltpu.VMEM((2 * TOK, TOK), F32),
        pltpu.VMEM((TOK, PW), F32),
        pltpu.VMEM((1024, 2 * PW), BF16),
        pltpu.VMEM((4, 8, 128), jnp.int32),
        pltpu.VMEM((8, 128), jnp.int32),
        pltpu.VMEM((2, 2, 384, PW), F32),
        pltpu.VMEM((subs, 384, PW), BF16),
        pltpu.VMEM((subs, 384, PW), BF16),
        pltpu.VMEM((2, 2, 96, PW), F32),
        pltpu.VMEM((96, PW), F32),
        pltpu.VMEM((subs, 3, 96, PW), BF16),
        pltpu.VMEM((subs, 3, 96, PW), BF16),
        pltpu.VMEM((2, 2, 24, PW), F32),
        pltpu.VMEM((subs, 3, 24, PW), F32),
        pltpu.VMEM((subs, 3, 24, PW), F32),
        pltpu.VMEM((24, PW), F32),
        pltpu.VMEM((subs, 4, 8, PW), F32),
        pltpu.VMEM((subs, 3, 8, PW), F32),
        dma((PAIRS,)),
        dma(()),
        dma((PAIRS, 5)),
        dma(()),
        dma((2,)),
        dma((2,)),
        dma((2, PAIRS)),
        dma((6, PAIRS)),
        dma((2, PAIRS)),
        dma((5, PAIRS)),
        dma((8, subs)),
    ]
    out, dq, dk, dv, dcq, dw = pl.pallas_call(
        kernel,
        out_shape=[slab] * 5 + [jax.ShapeDtypeStruct((8, 2 * HEADS * HD), F32)],
        in_specs=[any_spec] * 5 + [pl.BlockSpec(memory_space=pltpu.SMEM)] + [any_spec] * 3,
        out_specs=[any_spec] * 5 + [pl.BlockSpec(memory_space=pltpu.VMEM)],
        scratch_shapes=scratch,
        compiler_params=pltpu.CompilerParams(
            collective_id=0, has_side_effects=True, vmem_limit_bytes=60 * 1024 * 1024
        ),
        cost_estimate=pl.CostEstimate(flops=20_000_000_000, bytes_accessed=20_000_000, transcendentals=3_000_000),
    )(
        self_query[0],
        self_key[0],
        self_value[0],
        cross_query[0],
        neighbours.reshape(1024, ENC),
        neighbour_count,
        kv_weight,
        out_grad[0],
        jnp.asarray(row_orders()),
    )
    return out[None], dq[None], dk[None], dv[None], dcq[None], dw[:6]


def solution(mesh):
    in_specs = (
        P("fsdp", "seq", None),
        P("fsdp", "seq", None),
        P("fsdp", "seq", None),
        P("fsdp", "seq", None),
        P("fsdp", "seq", None, None),
        P("fsdp", "seq"),
        P("fsdp", None),
        P("fsdp", "seq", None),
    )
    out_specs = (
        P("fsdp", "seq", None),
        P("fsdp", "seq", None),
        P("fsdp", "seq", None),
        P("fsdp", "seq", None),
        P("fsdp", "seq", None),
        P(("seq", "fsdp"), None),
    )
    return jax.shard_map(
        on_device, mesh=mesh, in_specs=in_specs, out_specs=out_specs, check_vma=False
    )
```

```python
import jax
import jax.numpy as jnp
import numpy as np
from jax import lax
from jax.experimental import pallas as pl
from jax.experimental.pallas import tpu as pltpu
from jax.sharding import PartitionSpec as P

HEADS = 16
HD = 128
GROUP = 64
RLEN = 128
ENC = 768
TOK = 256
PAIRS = 8
PW = 256
SLABS = 32
SCALE = HD**-0.5
LOG2E = 1.4426950408889634
MESH_ID = pl.DeviceIdType.MESH
F32 = jnp.float32
BF16 = jnp.bfloat16

NN = (((1,), (0,)), ((), ()))
NT = (((1,), (1,)), ((), ()))
TN = (((0,), (0,)), ((), ()))


def dot(a, b, dims=NN):
    return lax.dot_general(a, b, dims, preferred_element_type=F32)


def row_orders():
    sizes = {"z": 4, "y": 4, "c": 2, "x": 4}
    grids = np.meshgrid(*[np.arange(n) for n in (2, 4, 4, 4, 6)], indexing="ij")
    out = np.zeros((3, ENC, ENC), np.float32)
    for t, axes in enumerate(("zyx", "yxz", "xzy")):
        at = {"c": grids[0], axes[0]: grids[1], axes[1]: grids[2], axes[2]: grids[3]}
        natural = (((at["z"] * sizes["y"] + at["y"]) * 2 + at["c"]) * 4 + at["x"]) * 6 + grids[4]
        out[t, np.arange(ENC), natural.reshape(-1)] = 1.0
    return out.astype(BF16)


def mod(a, n):
    return lax.rem(a, n)


def kernel(
    q_h, k_h, v_h, cq_h, nb_h, cnt_s, w_h, do_h, pt_h,
    out_o, dq_o, dk_o, dv_o, dcq_o, dw_o,
    qv, cqv, dov, kv, nbx, ptv, nbt, wv, kvret, kvsend, kvown, stage,
    bias, selfout, crossout, dkv, cntv, cntsend,
    own, csend, crecv, own1, t1, s1send, s1recv, own2, s2send, s2recv, own3, s3send, s3recv,
    load_sem, pt_sem, tok_sem, nb_sem, nbh_sem, cnt_sem, kvx_sem, w_sem, ret_sem, out_sem, rs_sem,
):
    s = lax.axis_index("seq")
    x = lax.axis_index("fsdp")
    c = mod(s, 2)
    y = mod(s // 2, 4)
    z = s // 8
    first = s == 0
    nxt = mod(s + 1, SLABS)
    prv = mod(s + SLABS - 1, SLABS)
    sib = s + 1 - 2 * c
    xr = mod(x + 1, 4)
    xl = mod(x + 3, 4)
    xa = mod(x + 2, 4)

    def seq_of(zz, yy):
        return (zz * 4 + yy) * 2 + c

    def dev(seq, fs):
        return {"seq": seq, "fsdp": fs}

    def remote(src, dst, ssem, rsem, where):
        return pltpu.make_async_remote_copy(
            src_ref=src, dst_ref=dst, send_sem=ssem, recv_sem=rsem, device_id=where, device_id_type=MESH_ID
        )

    def wait(ref, sem):
        pltpu.make_async_copy(ref, ref, sem).wait()

    def rows(start, size):
        return pl.ds(pl.multiple_of(start, 8), size)

    def cols(start, size):
        return pl.ds(pl.multiple_of(start, 128), size)

    barrier = pltpu.get_barrier_semaphore()
    partners = [dev(sib, x), dev(nxt, x), dev(prv, x)]
    for d in range(1, 4):
        partners += [dev(s, mod(x + d, 4)), dev(seq_of(z, mod(y + d, 4)), x), dev(seq_of(mod(z + d, 4), y), x)]
    for partner in partners:
        pl.semaphore_signal(barrier, inc=1, device_id=partner, device_id_type=MESH_ID)

    def load_w(p, _):
        for half in range(2):
            pltpu.make_async_copy(
                w_h.at[:, cols(half * 2048 + p * PW, PW)],
                wv.at[p, rows(x * 192, 192), pl.ds(half * PW, PW)],
                load_sem.at[p],
            ).start()
        return 0

    lax.fori_loop(0, PAIRS, load_w, 0)
    own_nb = pltpu.make_async_copy(nb_h.at[pl.ds(0, 768)], nbx.at[pl.ds(256, 768)], nb_sem)
    own_nb.start()
    pt_copy = pltpu.make_async_copy(pt_h, ptv, pt_sem)
    pt_copy.start()

    token_copies = [
        pltpu.make_async_copy(src, dst, tok_sem.at[n])
        for n, (src, dst) in enumerate(
            ((q_h, qv), (k_h, kv.at[0, pl.ds(256, 256)]), (v_h, kv.at[1, pl.ds(256, 256)]), (do_h, dov), (cq_h, cqv))
        )
    ]
    for copy in token_copies:
        copy.start()

    for g in range(3):
        cntv[g + 1] = jnp.full((8, 128), cnt_s[0, g], jnp.int32)
    cntsend[...] = jnp.full((8, 128), cnt_s[0, 3], jnp.int32)
    own3[...] = jnp.zeros(own3.shape, F32)

    pl.semaphore_wait(barrier, len(partners))

    def w_first(p):
        wait(wv.at[p, rows(x * 192, 192)], load_sem.at[p])
        piece = wv.at[p, rows(x * 192 + c * 96, 96)]
        for where in (xr, xl):
            remote(piece, piece, w_sem.at[0, p], w_sem.at[1, p], dev(s, where)).start()

    def w_second(p):
        wait(wv.at[p, pl.ds(0, 192)], w_sem.at[1, p])
        from_left = wv.at[p, rows(xl * 192 + c * 96, 48)]
        from_right = wv.at[p, rows(xr * 192 + c * 96 + 48, 48)]
        remote(from_left, from_left, w_sem.at[2, p], w_sem.at[3, p], dev(s, xr)).start()
        remote(from_right, from_right, w_sem.at[2, p], w_sem.at[3, p], dev(s, xl)).start()
        for shard in (xl, xr):
            piece = wv.at[p, rows(shard * 192 + c * 96, 96)]
            remote(piece, piece, w_sem.at[4, p], w_sem.at[5, p], dev(sib, x)).start()

    def w_third(p):
        wait(wv.at[p, pl.ds(0, 96)], w_sem.at[3, p])
        piece = wv.at[p, rows(xa * 192 + c * 96, 96)]
        remote(piece, piece, w_sem.at[4, p], w_sem.at[5, p], dev(sib, x)).start()

    def w_done(p):
        wait(wv.at[p, pl.ds(0, 288)], w_sem.at[5, p])

    w_first(0)
    halo = remote(nb_h.at[pl.ds(768, 256)], nbx.at[pl.ds(0, 256)], nbh_sem.at[0], nbh_sem.at[1], dev(nxt, x))
    halo.start()
    count_copy = remote(cntsend, cntv.at[0], cnt_sem.at[0], cnt_sem.at[1], dev(nxt, x))
    count_copy.start()

    def send_kv(p):
        span = cols(p * PW, PW)
        for n, src in enumerate((k_h, v_h)):
            remote(src.at[:, span], kv.at[n, pl.ds(0, 256), span], kvx_sem.at[0, p], kvx_sem.at[1, p], dev(nxt, x)).start()

    send_kv(0)
    w_first(1)
    send_kv(1)
    w_first(2)
    send_kv(2)

    key_at = lax.broadcasted_iota(jnp.int32, (384, 128), 0)
    query_at = lax.broadcasted_iota(jnp.int32, (384, 128), 1)
    for b in range(2):
        allowed = (key_at > query_at) & (key_at <= query_at + TOK)
        allowed = allowed & ((key_at + b * 128 >= TOK) | jnp.logical_not(first))
        bias[b] = jnp.where(allowed, 0.0, -1e30).astype(F32)

    pt_copy.wait()
    own_nb.wait()

    def reorder(n, _):
        t = n // 3
        g = mod(n, 3) + 1
        nbt[t, :, cols(g * 256, 256)] = dot(ptv[t], nbx[rows(g * 256, 256)], NT).astype(BF16)
        return 0

    lax.fori_loop(0, 9, reorder, 0)
    w_second(0)
    w_first(3)
    halo.wait_recv()

    def reorder_halo(t, _):
        nbt[t, :, pl.ds(0, 256)] = dot(ptv[t], nbx[pl.ds(0, 256)], NT).astype(BF16)
        return 0

    lax.fori_loop(0, 3, reorder_halo, 0)
    count_copy.wait_recv()
    w_third(0)
    w_second(1)
    for copy in token_copies:
        copy.wait()

    def softmax_grads(sc, dp):
        e = jnp.exp2(sc - jnp.max(sc, axis=0, keepdims=True))
        inv = 1.0 / jnp.sum(e, axis=0, keepdims=True)
        probs = e * inv
        delta = jnp.sum(e * dp, axis=0, keepdims=True) * inv
        return probs, probs * ((dp - delta) * SCALE)

    def self_pair(p):
        wait(kv.at[:, pl.ds(0, 256), cols(p * PW, PW)], kvx_sem.at[1, p])
        slot = mod(p, 4)
        zero = jnp.zeros((128, 128), BF16)
        for h in range(2):
            lanes = pl.ds(h * HD, HD)
            at = cols(p * PW + h * HD, HD)
            qh = qv[:, at]
            doh = dov[:, at]
            kh = kv[0, :, at]
            vh = kv[1, :, at]
            sc = dot(kh, qh, NT)
            dp = dot(vh, doh, NT)
            parts = []
            for b in range(2):
                near = slice(b * 128, b * 128 + 384)
                here = slice(b * 128, b * 128 + 128)
                probs, ds = softmax_grads(sc[near, here] * (SCALE * LOG2E) + bias[b], dp[near, here])
                parts.append((probs.astype(BF16), ds.astype(BF16)))
            for b, (probs, ds) in enumerate(parts):
                near = slice(b * 128, b * 128 + 384)
                selfout[p, pl.ds(b * 128, 128), lanes] = dot(probs, vh[near], TN)
                stage[1, pl.ds(b * 128, 128), at] = dot(ds, kh[near], TN).astype(BF16)

            def joined(n):
                return jnp.concatenate(
                    [jnp.concatenate([parts[0][n], zero], 0), jnp.concatenate([zero, parts[1][n]], 0)], 1
                )

            dv = dot(joined(0), doh)
            dk = dot(joined(1), qh)
            kvsend[p, 0, :, lanes] = dk[:TOK].astype(BF16)
            kvsend[p, 1, :, lanes] = dv[:TOK].astype(BF16)
            kvown[slot, 0, :, lanes] = dk[TOK:]
            kvown[slot, 1, :, lanes] = dv[TOK:]
        remote(kvsend.at[p], kvret.at[p], ret_sem.at[0, p], ret_sem.at[1, p], dev(prv, x)).start()
        write_out(1, dq_o, p)

    def write_out(n, dst, p):
        span = cols(p * PW, PW)
        pltpu.make_async_copy(stage.at[n, :, span], dst.at[:, span], out_sem.at[n, p]).start()

    def returned(p):
        wait(kvret.at[p], ret_sem.at[1, p])
        slot = mod(p, 4)
        for n, dst in enumerate((dk_o, dv_o)):
            stage[3 + n, :, cols(p * PW, PW)] = (kvown[slot, n] + kvret[p, n].astype(F32)).astype(BF16)
            write_out(3 + n, dst, p)

    def cross_pair(p):
        lane = lax.broadcasted_iota(jnp.int32, (GROUP, PW), 1)
        key_row = lax.broadcasted_iota(jnp.int32, (256, 128), 0)
        zero = jnp.zeros((GROUP, PW), BF16)
        span = cols(p * PW, PW)
        live = [jnp.where(first, 0.0, 1.0).astype(F32), None, None, None]

        def both(a):
            return jnp.concatenate([jnp.where(lane < HD, a, zero), jnp.where(lane >= HD, a, zero)], 0)

        def split(a):
            return jnp.concatenate([a[:GROUP, :HD], a[GROUP:, HD:]], 1)

        groups = range(4)
        toks = [pl.ds(g * GROUP, GROUP) for g in groups]
        proj = [dot(nbx[pl.ds(g * 256, 256)], wv[p]).astype(BF16) for g in groups]
        kp = [a[:, :PW] for a in proj]
        vp = [a[:, PW:] for a in proj]
        qb = [both(cqv[tok, span]) for tok in toks]
        dob = [both(dov[tok, span]) for tok in toks]
        sc = [dot(kp[g], qb[g], NT) for g in groups]
        dp = [dot(vp[g], dob[g], NT) for g in groups]
        low = []
        for g in groups:
            used = key_row < cntv[g, pl.ds(0, 1), :] * RLEN
            probs, ds = softmax_grads(jnp.where(used, sc[g] * (SCALE * LOG2E), -1e30), dp[g])
            if live[g] is not None:
                probs, ds = probs * live[g], ds * live[g]
            low.append((probs.astype(BF16), ds.astype(BF16)))
        for g, (probs, ds) in enumerate(low):
            dkv[pl.ds(g * 256, 256), pl.ds(0, PW)] = dot(ds, qb[g]).astype(BF16)
            dkv[pl.ds(g * 256, 256), pl.ds(PW, PW)] = dot(probs, dob[g]).astype(BF16)
        for g, (probs, ds) in enumerate(low):
            crossout[p, toks[g], :] = split(dot(probs, vp[g], TN))
            stage[2, toks[g], span] = split(dot(ds, kp[g], TN)).astype(BF16)
        write_out(2, dcq_o, p)

    def finish_out(p):
        span = cols(p * PW, PW)
        stage[0, :, span] = (selfout[p] + crossout[p]).astype(BF16)
        write_out(0, out_o, p)

    def kind(p, n):
        if n:
            return 1 + p // 4
        return mod(p, 4) // 2 * (1 - mod(p, 2)) * (2 - p // 4)

    def places(p, n):
        t = kind(p, n)
        a, b, e = (2 - t) // 2, mod(t, 2), t // 2
        return a * z + b * y + e * x, a * y + b * x + e * z, a * x + b * z + e * y

    def peer(p, n, order, d):
        t = kind(p, n)
        a, b, e = d * ((2 - t) // 2), d * mod(t, 2), d * (t // 2)
        dz, dy, dx = ((a, b, e), (e, a, b), (b, e, a))[order]
        return dev(seq_of(mod(z + dz, 4), mod(y + dy, 4)), mod(x + dx, 4))

    def weight_grad(p):
        slot = mod(p, 2)
        for n in range(2):
            u = 2 * p + n
            t = kind(p, n)
            grads = dkv[:, pl.ds(n * PW, PW)]
            csend[u] = dot(nbt[t, rows((1 - c) * 384, 384), :], grads).astype(BF16)
            remote(csend.at[u], crecv.at[u], rs_sem.at[0, u], rs_sem.at[1, u], dev(sib, x)).start()
        for n in range(2):
            u = 2 * p + n
            t = kind(p, n)
            grads = dkv[:, pl.ds(n * PW, PW)]
            own[slot, n] = dot(nbt[t, rows(c * 384, 384), :], grads)

    def rs_core(p, n):
        u = 2 * p + n
        slot = mod(p, 2)
        m1, _, _ = places(p, n)
        wait(crecv.at[u], rs_sem.at[1, u])
        for d in (2, 1, 3):
            span = rows(mod(m1 + d, 4) * 96, 96)
            s1send[u, d - 1] = (own[slot, n, span, :] + crecv[u, span, :].astype(F32)).astype(BF16)
            remote(s1send.at[u, d - 1], s1recv.at[u, d - 1], rs_sem.at[2, u], rs_sem.at[3, u], peer(p, n, 0, d)).start()
        span = rows(m1 * 96, 96)
        own1[p, n] = own[slot, n, span, :] + crecv[u, span, :].astype(F32)

    def rs_first(p, n):
        u = 2 * p + n
        slot = mod(p, 2)
        _, m2, _ = places(p, n)
        wait(s1recv.at[u], rs_sem.at[3, u])
        t1[...] = own1[p, n] + ((s1recv[u, 0].astype(F32) + s1recv[u, 1].astype(F32)) + s1recv[u, 2].astype(F32))
        for d in (2, 1, 3):
            piece = t1[rows(mod(m2 + d, 4) * 24, 24), :]
            s2send[u, d - 1] = jnp.concatenate([piece[:, :128], piece[:, 128:]], 0).astype(BF16)
            remote(s2send.at[u, d - 1], s2recv.at[u, d - 1], rs_sem.at[4, u], rs_sem.at[5, u], peer(p, n, 1, d)).start()
        own2[p, n] = t1[rows(m2 * 24, 24), :]

    def rs_second(p, n):
        u = 2 * p + n
        slot = mod(p, 2)
        _, _, m3 = places(p, n)
        wait(s2recv.at[u], rs_sem.at[5, u])
        got = [s2recv[u, d].astype(F32) for d in range(3)]
        got = (got[0] + got[1]) + got[2]
        total = own2[p, n] + jnp.concatenate([got[:24], got[24:]], 1)
        for a in range(4):
            piece = total[a * 6 : a * 6 + 6]
            own3[p, n, a, pl.ds(0, 6), :] = piece
            piece = jnp.concatenate([piece, jnp.zeros((2, PW), F32)], 0)
            s3send[u, a] = jnp.concatenate([piece[:, :128], piece[:, 128:]], 0).astype(BF16)
        for d in (2, 1, 3):
            remote(s3send.at[u, mod(m3 + d, 4)], s3recv.at[u, d - 1], rs_sem.at[6, u], rs_sem.at[7, u], peer(p, n, 2, d)).start()

    def rs_third(p, n):
        u = 2 * p + n
        _, _, m3 = places(p, n)
        wait(s3recv.at[u], rs_sem.at[7, u])
        got = [s3recv[u, d].astype(F32) for d in range(3)]
        got = (got[0] + got[1]) + got[2]
        dw_o[:, cols(n * 2048 + p * PW, PW)] = own3[p, n, m3] + jnp.concatenate([got[:8], got[8:]], 1)

    def step(i, _):
        @pl.when(i < PAIRS - 2)
        def _():
            w_second(i + 2)

        @pl.when(i < PAIRS - 3)
        def _():
            send_kv(i + 3)

        @pl.when(i < PAIRS - 4)
        def _():
            w_first(i + 4)

        @pl.when(i < PAIRS)
        def _():
            self_pair(i)

        @pl.when(i < PAIRS - 1)
        def _():
            w_third(i + 1)

        for lag, stage_of in ((1, rs_core), (3, rs_first), (5, rs_second), (7, rs_third)):

            @pl.when((i >= lag) & (i < PAIRS + lag))
            def _(lag=lag, stage_of=stage_of):
                for n in range(2):
                    stage_of(i - lag, n)

        @pl.when((i >= 3) & (i < PAIRS + 3))
        def _():
            returned(i - 3)

        @pl.when(i < PAIRS)
        def _():
            w_done(i)
            cross_pair(i)
            weight_grad(i)

            finish_out(i)

        return 0

    lax.fori_loop(0, PAIRS + 7, step, 0)

    halo.wait_send()
    count_copy.wait_send()

    def drain(p, _):
        wait(kv.at[:, pl.ds(0, 256), cols(p * PW, PW)], kvx_sem.at[0, p])
        wait(wv.at[p, pl.ds(0, 192)], w_sem.at[0, p])
        wait(wv.at[p, pl.ds(0, 96)], w_sem.at[2, p])
        wait(wv.at[p, pl.ds(0, 288)], w_sem.at[4, p])
        wait(kvsend.at[p], ret_sem.at[0, p])
        for n in range(5):
            wait(stage.at[n, :, cols(p * PW, PW)], out_sem.at[n, p])
        for n in range(2):
            u = 2 * p + n
            wait(csend.at[u], rs_sem.at[0, u])
            wait(s1send.at[u], rs_sem.at[2, u])
            wait(s2send.at[u], rs_sem.at[4, u])
            wait(s3recv.at[u], rs_sem.at[6, u])
        return 0

    lax.fori_loop(0, PAIRS, drain, 0)


def finish(*refs):
    ins, outs, slabs, tail, sem = refs[:6], refs[6:12], refs[12], refs[13], refs[14]
    held = [slabs.at[n] for n in range(5)] + [tail]
    reads = [pltpu.make_async_copy(a, b, sem.at[0, n]) for n, (a, b) in enumerate(zip(ins, held))]
    writes = [pltpu.make_async_copy(a, b, sem.at[1, n]) for n, (a, b) in enumerate(zip(held, outs))]
    for copy in reads:
        copy.start()
    for read, write in zip(reads, writes):
        read.wait()
        write.start()
    for copy in writes:
        copy.wait()


def on_device(
    self_query, self_key, self_value, cross_query, neighbours, neighbour_count, kv_weight, out_grad
):
    any_spec = pl.BlockSpec(memory_space=pl.ANY)
    slab = jax.ShapeDtypeStruct((TOK, HEADS * HD), BF16)
    dma = pltpu.SemaphoreType.DMA
    subs = 2 * PAIRS
    scratch = [
        pltpu.VMEM((TOK, HEADS * HD), BF16),
        pltpu.VMEM((TOK, HEADS * HD), BF16),
        pltpu.VMEM((TOK, HEADS * HD), BF16),
        pltpu.VMEM((2, 2 * TOK, HEADS * HD), BF16),
        pltpu.VMEM((1024, ENC), BF16),
        pltpu.VMEM((3, ENC, ENC), BF16),
        pltpu.VMEM((3, ENC, 1024), BF16),
        pltpu.VMEM((PAIRS, ENC, 2 * PW), BF16),
        pltpu.VMEM((PAIRS, 2, TOK, PW), BF16),
        pltpu.VMEM((PAIRS, 2, TOK, PW), BF16),
        pltpu.VMEM((4, 2, TOK, PW), F32),
        pltpu.VMEM((5, TOK, HEADS * HD), BF16),
        pltpu.VMEM((2, 384, 128), F32),
        pltpu.VMEM((PAIRS, TOK, PW), F32),
        pltpu.VMEM((PAIRS, TOK, PW), F32),
        pltpu.VMEM((1024, 2 * PW), BF16),
        pltpu.VMEM((4, 8, 128), jnp.int32),
        pltpu.VMEM((8, 128), jnp.int32),
        pltpu.VMEM((2, 2, 384, PW), F32),
        pltpu.VMEM((subs, 384, PW), BF16),
        pltpu.VMEM((subs, 384, PW), BF16),
        pltpu.VMEM((PAIRS, 2, 96, PW), F32),
        pltpu.VMEM((96, PW), F32),
        pltpu.VMEM((subs, 3, 96, PW), BF16),
        pltpu.VMEM((subs, 3, 96, PW), BF16),
        pltpu.VMEM((PAIRS, 2, 24, PW), F32),
        pltpu.VMEM((subs, 3, 48, 128), BF16),
        pltpu.VMEM((subs, 3, 48, 128), BF16),
        pltpu.VMEM((PAIRS, 2, 4, 8, PW), F32),
        pltpu.VMEM((subs, 4, 16, 128), BF16),
        pltpu.VMEM((subs, 3, 16, 128), BF16),
        dma((PAIRS,)),
        dma(()),
        dma((5,)),
        dma(()),
        dma((2,)),
        dma((2,)),
        dma((2, PAIRS)),
        dma((6, PAIRS)),
        dma((2, PAIRS)),
        dma((5, PAIRS)),
        dma((8, subs)),
    ]
    out, dq, dk, dv, dcq, dw = pl.pallas_call(
        kernel,
        out_shape=[slab] * 5 + [jax.ShapeDtypeStruct((8, 2 * HEADS * HD), F32)],
        in_specs=[any_spec] * 5 + [pl.BlockSpec(memory_space=pltpu.SMEM)] + [any_spec] * 3,
        out_specs=[any_spec] * 5 + [pl.BlockSpec(memory_space=pltpu.VMEM)],
        scratch_shapes=scratch,
        compiler_params=pltpu.CompilerParams(
            collective_id=0, has_side_effects=True, vmem_limit_bytes=60 * 1024 * 1024
        ),
        cost_estimate=pl.CostEstimate(flops=20_000_000_000, bytes_accessed=20_000_000, transcendentals=3_000_000),
    )(
        self_query[0],
        self_key[0],
        self_value[0],
        cross_query[0],
        neighbours.reshape(1024, ENC),
        neighbour_count,
        kv_weight,
        out_grad[0],
        jnp.asarray(row_orders()),
    )
    out, dq, dk, dv, dcq, dw = pl.pallas_call(
        finish,
        out_shape=[slab] * 5 + [jax.ShapeDtypeStruct((8, 2 * HEADS * HD), F32)],
        in_specs=[any_spec] * 6,
        out_specs=[any_spec] * 6,
        scratch_shapes=[
            pltpu.VMEM((5, TOK, HEADS * HD), BF16),
            pltpu.VMEM((8, 2 * HEADS * HD), F32),
            dma((2, 6)),
        ],
        cost_estimate=pl.CostEstimate(flops=0, bytes_accessed=10_000_000, transcendentals=0),
    )(out, dq, dk, dv, dcq, dw)
    return out[None], dq[None], dk[None], dv[None], dcq[None], dw[:6]


def solution(mesh):
    in_specs = (
        P("fsdp", "seq", None),
        P("fsdp", "seq", None),
        P("fsdp", "seq", None),
        P("fsdp", "seq", None),
        P("fsdp", "seq", None, None),
        P("fsdp", "seq"),
        P("fsdp", None),
        P("fsdp", "seq", None),
    )
    out_specs = (
        P("fsdp", "seq", None),
        P("fsdp", "seq", None),
        P("fsdp", "seq", None),
        P("fsdp", "seq", None),
        P("fsdp", "seq", None),
        P(("seq", "fsdp"), None),
    )
    return jax.shard_map(
        on_device, mesh=mesh, in_specs=in_specs, out_specs=out_specs, check_vma=False
    )
```

```python
import jax
import jax.numpy as jnp
import numpy as np
from jax import lax
from jax.experimental import pallas as pl
from jax.experimental.pallas import tpu as pltpu
from jax.sharding import PartitionSpec as P

HEADS = 16
HD = 128
GROUP = 64
RLEN = 128
ENC = 768
TOK = 256
PAIRS = 8
PW = 256
SLABS = 32
SCALE = HD**-0.5
LOG2E = 1.4426950408889634
MESH_ID = pl.DeviceIdType.MESH
F32 = jnp.float32
BF16 = jnp.bfloat16

NN = (((1,), (0,)), ((), ()))
NT = (((1,), (1,)), ((), ()))
TN = (((0,), (0,)), ((), ()))


def dot(a, b, dims=NN):
    return lax.dot_general(a, b, dims, preferred_element_type=F32)


def row_orders():
    sizes = {"z": 4, "y": 4, "c": 2, "x": 4}
    grids = np.meshgrid(*[np.arange(n) for n in (2, 4, 4, 4, 6)], indexing="ij")
    out = np.zeros((3, ENC, ENC), np.float32)
    for t, axes in enumerate(("zyx", "yxz", "xzy")):
        at = {"c": grids[0], axes[0]: grids[1], axes[1]: grids[2], axes[2]: grids[3]}
        natural = (((at["z"] * sizes["y"] + at["y"]) * 2 + at["c"]) * 4 + at["x"]) * 6 + grids[4]
        out[t, np.arange(ENC), natural.reshape(-1)] = 1.0
    return out.astype(BF16)


def mod(a, n):
    return lax.rem(a, n)


def kernel(
    q_h, k_h, v_h, cq_h, nb_h, cnt_s, w_h, do_h, pt_h,
    out_o, dq_o, dk_o, dv_o, dcq_o, dw_o,
    qv, cqv, dov, kv, nbx, ptv, nbt, wv, kvret, kvsend, kvown, stage,
    bias, selfout, crossout, dkv, cntv, cntsend,
    own, csend, crecv, own1, t1, s1send, s1recv, own2, s2send, s2recv, own3, s3send, s3recv,
    load_sem, pt_sem, tok_sem, nb_sem, nbh_sem, cnt_sem, kvx_sem, w_sem, ret_sem, out_sem, rs_sem,
):
    s = lax.axis_index("seq")
    x = lax.axis_index("fsdp")
    c = mod(s, 2)
    y = mod(s // 2, 4)
    z = s // 8
    first = s == 0
    nxt = mod(s + 1, SLABS)
    prv = mod(s + SLABS - 1, SLABS)
    sib = s + 1 - 2 * c
    xr = mod(x + 1, 4)
    xl = mod(x + 3, 4)
    xa = mod(x + 2, 4)

    def seq_of(zz, yy):
        return (zz * 4 + yy) * 2 + c

    def dev(seq, fs):
        return {"seq": seq, "fsdp": fs}

    def remote(src, dst, ssem, rsem, where):
        return pltpu.make_async_remote_copy(
            src_ref=src, dst_ref=dst, send_sem=ssem, recv_sem=rsem, device_id=where, device_id_type=MESH_ID
        )

    def wait(ref, sem):
        pltpu.make_async_copy(ref, ref, sem).wait()

    def rows(start, size):
        return pl.ds(pl.multiple_of(start, 8), size)

    def cols(start, size):
        return pl.ds(pl.multiple_of(start, 128), size)

    barrier = pltpu.get_barrier_semaphore()
    partners = [dev(sib, x), dev(nxt, x), dev(prv, x)]
    for d in range(1, 4):
        partners += [dev(s, mod(x + d, 4)), dev(seq_of(z, mod(y + d, 4)), x), dev(seq_of(mod(z + d, 4), y), x)]
    for partner in partners:
        pl.semaphore_signal(barrier, inc=1, device_id=partner, device_id_type=MESH_ID)

    def load_w(p, _):
        for half in range(2):
            pltpu.make_async_copy(
                w_h.at[:, cols(half * 2048 + p * PW, PW)],
                wv.at[p, rows(x * 192, 192), pl.ds(half * PW, PW)],
                load_sem.at[p],
            ).start()
        return 0

    lax.fori_loop(0, PAIRS, load_w, 0)
    own_nb = pltpu.make_async_copy(nb_h.at[pl.ds(0, 768)], nbx.at[pl.ds(256, 768)], nb_sem)
    own_nb.start()
    pt_copy = pltpu.make_async_copy(pt_h, ptv, pt_sem)
    pt_copy.start()

    token_copies = [
        pltpu.make_async_copy(src, dst, tok_sem.at[n])
        for n, (src, dst) in enumerate(
            ((q_h, qv), (k_h, kv.at[0, pl.ds(256, 256)]), (v_h, kv.at[1, pl.ds(256, 256)]), (do_h, dov), (cq_h, cqv))
        )
    ]
    for copy in token_copies:
        copy.start()

    for g in range(3):
        cntv[g + 1] = jnp.full((8, 128), cnt_s[0, g], jnp.int32)
    cntsend[...] = jnp.full((8, 128), cnt_s[0, 3], jnp.int32)
    own3[...] = jnp.zeros(own3.shape, F32)

    pl.semaphore_wait(barrier, len(partners))

    def w_first(p):
        wait(wv.at[p, rows(x * 192, 192)], load_sem.at[p])
        piece = wv.at[p, rows(x * 192 + c * 96, 96)]
        for where in (xr, xl):
            remote(piece, piece, w_sem.at[0, p], w_sem.at[1, p], dev(s, where)).start()

    def w_second(p):
        wait(wv.at[p, pl.ds(0, 192)], w_sem.at[1, p])
        from_left = wv.at[p, rows(xl * 192 + c * 96, 48)]
        from_right = wv.at[p, rows(xr * 192 + c * 96 + 48, 48)]
        remote(from_left, from_left, w_sem.at[2, p], w_sem.at[3, p], dev(s, xr)).start()
        remote(from_right, from_right, w_sem.at[2, p], w_sem.at[3, p], dev(s, xl)).start()
        for shard in (xl, xr):
            piece = wv.at[p, rows(shard * 192 + c * 96, 96)]
            remote(piece, piece, w_sem.at[4, p], w_sem.at[5, p], dev(sib, x)).start()

    def w_third(p):
        wait(wv.at[p, pl.ds(0, 96)], w_sem.at[3, p])
        piece = wv.at[p, rows(xa * 192 + c * 96, 96)]
        remote(piece, piece, w_sem.at[4, p], w_sem.at[5, p], dev(sib, x)).start()

    def w_done(p):
        wait(wv.at[p, pl.ds(0, 288)], w_sem.at[5, p])

    w_first(0)
    halo = remote(nb_h.at[pl.ds(768, 256)], nbx.at[pl.ds(0, 256)], nbh_sem.at[0], nbh_sem.at[1], dev(nxt, x))
    halo.start()
    count_copy = remote(cntsend, cntv.at[0], cnt_sem.at[0], cnt_sem.at[1], dev(nxt, x))
    count_copy.start()

    def send_kv(p):
        span = cols(p * PW, PW)
        for n, src in enumerate((k_h, v_h)):
            remote(src.at[:, span], kv.at[n, pl.ds(0, 256), span], kvx_sem.at[0, p], kvx_sem.at[1, p], dev(nxt, x)).start()

    send_kv(0)
    w_first(1)
    send_kv(1)
    w_first(2)
    send_kv(2)

    key_at = lax.broadcasted_iota(jnp.int32, (384, 128), 0)
    query_at = lax.broadcasted_iota(jnp.int32, (384, 128), 1)
    for b in range(2):
        allowed = (key_at > query_at) & (key_at <= query_at + TOK)
        allowed = allowed & ((key_at + b * 128 >= TOK) | jnp.logical_not(first))
        bias[b] = jnp.where(allowed, 0.0, -1e30).astype(F32)

    pt_copy.wait()
    own_nb.wait()

    def reorder(n, _):
        t = n // 3
        g = mod(n, 3) + 1
        nbt[t, :, cols(g * 256, 256)] = dot(ptv[t], nbx[rows(g * 256, 256)], NT).astype(BF16)
        return 0

    lax.fori_loop(0, 9, reorder, 0)
    w_second(0)
    w_first(3)
    halo.wait_recv()

    def reorder_halo(t, _):
        nbt[t, :, pl.ds(0, 256)] = dot(ptv[t], nbx[pl.ds(0, 256)], NT).astype(BF16)
        return 0

    lax.fori_loop(0, 3, reorder_halo, 0)
    count_copy.wait_recv()
    w_third(0)
    w_second(1)
    for copy in token_copies:
        copy.wait()

    def softmax_grads(sc, dp):
        e = jnp.exp2(sc - jnp.max(sc, axis=0, keepdims=True))
        inv = 1.0 / jnp.sum(e, axis=0, keepdims=True)
        probs = e * inv
        delta = jnp.sum(e * dp, axis=0, keepdims=True) * inv
        return probs, probs * ((dp - delta) * SCALE)

    def self_pair(p):
        wait(kv.at[:, pl.ds(0, 256), cols(p * PW, PW)], kvx_sem.at[1, p])
        slot = p
        zero = jnp.zeros((128, 128), BF16)
        for h in range(2):
            lanes = pl.ds(h * HD, HD)
            at = cols(p * PW + h * HD, HD)
            qh = qv[:, at]
            doh = dov[:, at]
            kh = kv[0, :, at]
            vh = kv[1, :, at]
            sc = dot(kh, qh, NT)
            dp = dot(vh, doh, NT)
            parts = []
            for b in range(2):
                near = slice(b * 128, b * 128 + 384)
                here = slice(b * 128, b * 128 + 128)
                probs, ds = softmax_grads(sc[near, here] * (SCALE * LOG2E) + bias[b], dp[near, here])
                parts.append((probs.astype(BF16), ds.astype(BF16)))
            for b, (probs, ds) in enumerate(parts):
                near = slice(b * 128, b * 128 + 384)
                selfout[p, pl.ds(b * 128, 128), lanes] = dot(probs, vh[near], TN)
                stage[1, pl.ds(b * 128, 128), at] = dot(ds, kh[near], TN).astype(BF16)

            def joined(n):
                return jnp.concatenate(
                    [jnp.concatenate([parts[0][n], zero], 0), jnp.concatenate([zero, parts[1][n]], 0)], 1
                )

            dv = dot(joined(0), doh)
            dk = dot(joined(1), qh)
            kvsend[p, 0, :, lanes] = dk[:TOK].astype(BF16)
            kvsend[p, 1, :, lanes] = dv[:TOK].astype(BF16)
            kvown[slot, 0, :, lanes] = dk[TOK:]
            kvown[slot, 1, :, lanes] = dv[TOK:]
        remote(kvsend.at[p], kvret.at[p], ret_sem.at[0, p], ret_sem.at[1, p], dev(prv, x)).start()
        write_out(1, dq_o, p)

    def write_out(n, dst, p):
        span = cols(p * PW, PW)
        pltpu.make_async_copy(stage.at[n, :, span], dst.at[:, span], out_sem.at[n, p]).start()

    def returned(p):
        wait(kvret.at[p], ret_sem.at[1, p])
        slot = p
        for n, dst in enumerate((dk_o, dv_o)):
            stage[3 + n, :, cols(p * PW, PW)] = (kvown[slot, n] + kvret[p, n].astype(F32)).astype(BF16)
            write_out(3 + n, dst, p)

    def cross_pair(p):
        lane = lax.broadcasted_iota(jnp.int32, (GROUP, PW), 1)
        key_row = lax.broadcasted_iota(jnp.int32, (256, 128), 0)
        zero = jnp.zeros((GROUP, PW), BF16)
        span = cols(p * PW, PW)
        live = [jnp.where(first, 0.0, 1.0).astype(F32), None, None, None]

        def both(a):
            return jnp.concatenate([jnp.where(lane < HD, a, zero), jnp.where(lane >= HD, a, zero)], 0)

        def split(a):
            return jnp.concatenate([a[:GROUP, :HD], a[GROUP:, HD:]], 1)

        groups = range(4)
        toks = [pl.ds(g * GROUP, GROUP) for g in groups]
        proj = [dot(nbx[pl.ds(g * 256, 256)], wv[p]).astype(BF16) for g in groups]
        kp = [a[:, :PW] for a in proj]
        vp = [a[:, PW:] for a in proj]
        qb = [both(cqv[tok, span]) for tok in toks]
        dob = [both(dov[tok, span]) for tok in toks]
        sc = [dot(kp[g], qb[g], NT) for g in groups]
        dp = [dot(vp[g], dob[g], NT) for g in groups]
        low = []
        for g in groups:
            used = key_row < cntv[g, pl.ds(0, 1), :] * RLEN
            probs, ds = softmax_grads(jnp.where(used, sc[g] * (SCALE * LOG2E), -1e30), dp[g])
            if live[g] is not None:
                probs, ds = probs * live[g], ds * live[g]
            low.append((probs.astype(BF16), ds.astype(BF16)))
        for g, (probs, ds) in enumerate(low):
            dkv[pl.ds(g * 256, 256), pl.ds(0, PW)] = dot(ds, qb[g]).astype(BF16)
            dkv[pl.ds(g * 256, 256), pl.ds(PW, PW)] = dot(probs, dob[g]).astype(BF16)
        for g, (probs, ds) in enumerate(low):
            crossout[p, toks[g], :] = split(dot(probs, vp[g], TN))
            stage[2, toks[g], span] = split(dot(ds, kp[g], TN)).astype(BF16)
        write_out(2, dcq_o, p)

    def finish_out(p):
        span = cols(p * PW, PW)
        stage[0, :, span] = (selfout[p] + crossout[p]).astype(BF16)
        write_out(0, out_o, p)

    def kind(p, n):
        if n:
            return 1 + p // 4
        return mod(p, 4) // 2 * (1 - mod(p, 2)) * (2 - p // 4)

    def places(p, n):
        t = kind(p, n)
        a, b, e = (2 - t) // 2, mod(t, 2), t // 2
        return a * z + b * y + e * x, a * y + b * x + e * z, a * x + b * z + e * y

    def peer(p, n, order, d):
        t = kind(p, n)
        a, b, e = d * ((2 - t) // 2), d * mod(t, 2), d * (t // 2)
        dz, dy, dx = ((a, b, e), (e, a, b), (b, e, a))[order]
        return dev(seq_of(mod(z + dz, 4), mod(y + dy, 4)), mod(x + dx, 4))

    def weight_grad(p):
        slot = mod(p, 2)
        for n in range(2):
            u = 2 * p + n
            t = kind(p, n)
            grads = dkv[:, pl.ds(n * PW, PW)]
            csend[u] = dot(nbt[t, rows((1 - c) * 384, 384), :], grads).astype(BF16)
            remote(csend.at[u], crecv.at[u], rs_sem.at[0, u], rs_sem.at[1, u], dev(sib, x)).start()
        for n in range(2):
            u = 2 * p + n
            t = kind(p, n)
            grads = dkv[:, pl.ds(n * PW, PW)]
            own[slot, n] = dot(nbt[t, rows(c * 384, 384), :], grads)

    def rs_core(p, n):
        u = 2 * p + n
        slot = mod(p, 2)
        m1, _, _ = places(p, n)
        wait(crecv.at[u], rs_sem.at[1, u])
        for d in (2, 1, 3):
            span = rows(mod(m1 + d, 4) * 96, 96)
            s1send[u, d - 1] = (own[slot, n, span, :] + crecv[u, span, :].astype(F32)).astype(BF16)
            remote(s1send.at[u, d - 1], s1recv.at[u, d - 1], rs_sem.at[2, u], rs_sem.at[3, u], peer(p, n, 0, d)).start()
        span = rows(m1 * 96, 96)
        own1[p, n] = own[slot, n, span, :] + crecv[u, span, :].astype(F32)

    def rs_first(p, n):
        u = 2 * p + n
        slot = mod(p, 2)
        _, m2, _ = places(p, n)
        wait(s1recv.at[u], rs_sem.at[3, u])
        t1[...] = own1[p, n] + ((s1recv[u, 0].astype(F32) + s1recv[u, 1].astype(F32)) + s1recv[u, 2].astype(F32))
        for d in (2, 1, 3):
            piece = t1[rows(mod(m2 + d, 4) * 24, 24), :]
            s2send[u, d - 1] = jnp.concatenate([piece[:, :128], piece[:, 128:]], 0).astype(BF16)
            remote(s2send.at[u, d - 1], s2recv.at[u, d - 1], rs_sem.at[4, u], rs_sem.at[5, u], peer(p, n, 1, d)).start()
        own2[p, n] = t1[rows(m2 * 24, 24), :]

    def rs_second(p, n):
        u = 2 * p + n
        slot = mod(p, 2)
        _, _, m3 = places(p, n)
        wait(s2recv.at[u], rs_sem.at[5, u])
        got = [s2recv[u, d].astype(F32) for d in range(3)]
        got = (got[0] + got[1]) + got[2]
        total = own2[p, n] + jnp.concatenate([got[:24], got[24:]], 1)
        for a in range(4):
            piece = total[a * 6 : a * 6 + 6]
            own3[p, n, a, pl.ds(0, 6), :] = piece
            piece = jnp.concatenate([piece, jnp.zeros((2, PW), F32)], 0)
            s3send[u, a] = jnp.concatenate([piece[:, :128], piece[:, 128:]], 0).astype(BF16)
        for d in (2, 1, 3):
            remote(s3send.at[u, mod(m3 + d, 4)], s3recv.at[u, d - 1], rs_sem.at[6, u], rs_sem.at[7, u], peer(p, n, 2, d)).start()

    def rs_third(p, n):
        u = 2 * p + n
        _, _, m3 = places(p, n)
        wait(s3recv.at[u], rs_sem.at[7, u])
        got = [s3recv[u, d].astype(F32) for d in range(3)]
        got = (got[0] + got[1]) + got[2]
        dw_o[:, cols(n * 2048 + p * PW, PW)] = own3[p, n, m3] + jnp.concatenate([got[:8], got[8:]], 1)

    def step(i, _):
        @pl.when(i < PAIRS - 2)
        def _():
            w_second(i + 2)

        @pl.when(i < PAIRS - 3)
        def _():
            send_kv(i + 3)

        @pl.when(i < PAIRS - 4)
        def _():
            w_first(i + 4)

        @pl.when(i < PAIRS - 1)
        def _():
            self_pair(i)
            w_third(i + 1)

        for lag, stage_of in ((1, rs_core), (3, rs_first), (5, rs_second), (7, rs_third)):

            @pl.when((i >= lag) & (i < PAIRS + lag))
            def _(lag=lag, stage_of=stage_of):
                for n in range(2):
                    stage_of(i - lag, n)

        @pl.when(i < PAIRS)
        def _():
            w_done(i)
            cross_pair(i)
            weight_grad(i)

        @pl.when(i == PAIRS)
        def _():
            self_pair(PAIRS - 1)

        @pl.when(i >= PAIRS - 1)
        def _():
            finish_out(i - PAIRS + 1)
            returned(i - PAIRS + 1)

        return 0

    lax.fori_loop(0, PAIRS + 7, step, 0)

    halo.wait_send()
    count_copy.wait_send()

    def drain(p, _):
        wait(kv.at[:, pl.ds(0, 256), cols(p * PW, PW)], kvx_sem.at[0, p])
        wait(wv.at[p, pl.ds(0, 192)], w_sem.at[0, p])
        wait(wv.at[p, pl.ds(0, 96)], w_sem.at[2, p])
        wait(wv.at[p, pl.ds(0, 288)], w_sem.at[4, p])
        wait(kvsend.at[p], ret_sem.at[0, p])
        for n in range(5):
            wait(stage.at[n, :, cols(p * PW, PW)], out_sem.at[n, p])
        for n in range(2):
            u = 2 * p + n
            wait(csend.at[u], rs_sem.at[0, u])
            wait(s1send.at[u], rs_sem.at[2, u])
            wait(s2send.at[u], rs_sem.at[4, u])
            wait(s3recv.at[u], rs_sem.at[6, u])
        return 0

    lax.fori_loop(0, PAIRS, drain, 0)


def finish(*refs):
    ins, outs, slabs, tail, sem = refs[:6], refs[6:12], refs[12], refs[13], refs[14]
    held = [slabs.at[n] for n in range(5)] + [tail]
    reads = [pltpu.make_async_copy(a, b, sem.at[0, n]) for n, (a, b) in enumerate(zip(ins, held))]
    writes = [pltpu.make_async_copy(a, b, sem.at[1, n]) for n, (a, b) in enumerate(zip(held, outs))]
    for copy in reads:
        copy.start()
    for read, write in zip(reads, writes):
        read.wait()
        write.start()
    for copy in writes:
        copy.wait()


def on_device(
    self_query, self_key, self_value, cross_query, neighbours, neighbour_count, kv_weight, out_grad
):
    any_spec = pl.BlockSpec(memory_space=pl.ANY)
    slab = jax.ShapeDtypeStruct((TOK, HEADS * HD), BF16)
    dma = pltpu.SemaphoreType.DMA
    subs = 2 * PAIRS
    scratch = [
        pltpu.VMEM((TOK, HEADS * HD), BF16),
        pltpu.VMEM((TOK, HEADS * HD), BF16),
        pltpu.VMEM((TOK, HEADS * HD), BF16),
        pltpu.VMEM((2, 2 * TOK, HEADS * HD), BF16),
        pltpu.VMEM((1024, ENC), BF16),
        pltpu.VMEM((3, ENC, ENC), BF16),
        pltpu.VMEM((3, ENC, 1024), BF16),
        pltpu.VMEM((PAIRS, ENC, 2 * PW), BF16),
        pltpu.VMEM((PAIRS, 2, TOK, PW), BF16),
        pltpu.VMEM((PAIRS, 2, TOK, PW), BF16),
        pltpu.VMEM((PAIRS, 2, TOK, PW), F32),
        pltpu.VMEM((5, TOK, HEADS * HD), BF16),
        pltpu.VMEM((2, 384, 128), F32),
        pltpu.VMEM((PAIRS, TOK, PW), F32),
        pltpu.VMEM((PAIRS, TOK, PW), F32),
        pltpu.VMEM((1024, 2 * PW), BF16),
        pltpu.VMEM((4, 8, 128), jnp.int32),
        pltpu.VMEM((8, 128), jnp.int32),
        pltpu.VMEM((2, 2, 384, PW), F32),
        pltpu.VMEM((subs, 384, PW), BF16),
        pltpu.VMEM((subs, 384, PW), BF16),
        pltpu.VMEM((PAIRS, 2, 96, PW), F32),
        pltpu.VMEM((96, PW), F32),
        pltpu.VMEM((subs, 3, 96, PW), BF16),
        pltpu.VMEM((subs, 3, 96, PW), BF16),
        pltpu.VMEM((PAIRS, 2, 24, PW), F32),
        pltpu.VMEM((subs, 3, 48, 128), BF16),
        pltpu.VMEM((subs, 3, 48, 128), BF16),
        pltpu.VMEM((PAIRS, 2, 4, 8, PW), F32),
        pltpu.VMEM((subs, 4, 16, 128), BF16),
        pltpu.VMEM((subs, 3, 16, 128), BF16),
        dma((PAIRS,)),
        dma(()),
        dma((5,)),
        dma(()),
        dma((2,)),
        dma((2,)),
        dma((2, PAIRS)),
        dma((6, PAIRS)),
        dma((2, PAIRS)),
        dma((5, PAIRS)),
        dma((8, subs)),
    ]
    out, dq, dk, dv, dcq, dw = pl.pallas_call(
        kernel,
        out_shape=[slab] * 5 + [jax.ShapeDtypeStruct((8, 2 * HEADS * HD), F32)],
        in_specs=[any_spec] * 5 + [pl.BlockSpec(memory_space=pltpu.SMEM)] + [any_spec] * 3,
        out_specs=[any_spec] * 5 + [pl.BlockSpec(memory_space=pltpu.VMEM)],
        scratch_shapes=scratch,
        compiler_params=pltpu.CompilerParams(
            collective_id=0, has_side_effects=True, vmem_limit_bytes=60 * 1024 * 1024
        ),
        cost_estimate=pl.CostEstimate(flops=20_000_000_000, bytes_accessed=20_000_000, transcendentals=3_000_000),
    )(
        self_query[0],
        self_key[0],
        self_value[0],
        cross_query[0],
        neighbours.reshape(1024, ENC),
        neighbour_count,
        kv_weight,
        out_grad[0],
        jnp.asarray(row_orders()),
    )
    out, dq, dk, dv, dcq, dw = pl.pallas_call(
        finish,
        out_shape=[slab] * 5 + [jax.ShapeDtypeStruct((8, 2 * HEADS * HD), F32)],
        in_specs=[any_spec] * 6,
        out_specs=[any_spec] * 6,
        scratch_shapes=[
            pltpu.VMEM((5, TOK, HEADS * HD), BF16),
            pltpu.VMEM((8, 2 * HEADS * HD), F32),
            dma((2, 6)),
        ],
        cost_estimate=pl.CostEstimate(flops=0, bytes_accessed=10_000_000, transcendentals=0),
    )(out, dq, dk, dv, dcq, dw)
    return out[None], dq[None], dk[None], dv[None], dcq[None], dw[:6]


def solution(mesh):
    in_specs = (
        P("fsdp", "seq", None),
        P("fsdp", "seq", None),
        P("fsdp", "seq", None),
        P("fsdp", "seq", None),
        P("fsdp", "seq", None, None),
        P("fsdp", "seq"),
        P("fsdp", None),
        P("fsdp", "seq", None),
    )
    out_specs = (
        P("fsdp", "seq", None),
        P("fsdp", "seq", None),
        P("fsdp", "seq", None),
        P("fsdp", "seq", None),
        P("fsdp", "seq", None),
        P(("seq", "fsdp"), None),
    )
    return jax.shard_map(
        on_device, mesh=mesh, in_specs=in_specs, out_specs=out_specs, check_vma=False
    )
```

```python
import jax
import jax.numpy as jnp
import numpy as np
from jax import lax
from jax.experimental import pallas as pl
from jax.experimental.pallas import tpu as pltpu
from jax.sharding import PartitionSpec as P

HEADS = 16
HD = 128
GROUP = 64
RLEN = 128
ENC = 768
TOK = 256
PAIRS = 8
PW = 256
SLABS = 32
SCALE = HD**-0.5
LOG2E = 1.4426950408889634
MESH_ID = pl.DeviceIdType.MESH
F32 = jnp.float32
BF16 = jnp.bfloat16

NN = (((1,), (0,)), ((), ()))
NT = (((1,), (1,)), ((), ()))
TN = (((0,), (0,)), ((), ()))


def dot(a, b, dims=NN):
    return lax.dot_general(a, b, dims, preferred_element_type=F32)


def row_orders():
    sizes = {"z": 4, "y": 4, "c": 2, "x": 4}
    grids = np.meshgrid(*[np.arange(n) for n in (2, 4, 4, 4, 6)], indexing="ij")
    out = np.zeros((3, ENC, ENC), np.float32)
    for t, axes in enumerate(("zyx", "yxz", "xzy")):
        at = {"c": grids[0], axes[0]: grids[1], axes[1]: grids[2], axes[2]: grids[3]}
        natural = (((at["z"] * sizes["y"] + at["y"]) * 2 + at["c"]) * 4 + at["x"]) * 6 + grids[4]
        out[t, np.arange(ENC), natural.reshape(-1)] = 1.0
    return out.astype(BF16)


def mod(a, n):
    return lax.rem(a, n)


def kernel(
    q_h, k_h, v_h, cq_h, nb_h, cnt_s, w_h, do_h, pt_h,
    out_o, dq_o, dk_o, dv_o, dcq_o, dw_o,
    qv, cqv, dov, kv, nbx, ptv, nbt, wv, kvret, kvsend, kvown, stage,
    bias, selfout, crossout, dkv, cntv, cntsend,
    own, csend, crecv, own1, t1, s1send, s1recv, own2, s2send, s2recv, own3, s3send, s3recv,
    load_sem, pt_sem, tok_sem, nb_sem, nbh_sem, cnt_sem, kvx_sem, w_sem, ret_sem, out_sem, rs_sem,
):
    s = lax.axis_index("seq")
    x = lax.axis_index("fsdp")
    c = mod(s, 2)
    y = mod(s // 2, 4)
    z = s // 8
    first = s == 0
    nxt = mod(s + 1, SLABS)
    prv = mod(s + SLABS - 1, SLABS)
    sib = s + 1 - 2 * c
    xr = mod(x + 1, 4)
    xl = mod(x + 3, 4)
    xa = mod(x + 2, 4)

    def seq_of(zz, yy):
        return (zz * 4 + yy) * 2 + c

    def dev(seq, fs):
        return {"seq": seq, "fsdp": fs}

    def remote(src, dst, ssem, rsem, where):
        return pltpu.make_async_remote_copy(
            src_ref=src, dst_ref=dst, send_sem=ssem, recv_sem=rsem, device_id=where, device_id_type=MESH_ID
        )

    def wait(ref, sem):
        pltpu.make_async_copy(ref, ref, sem).wait()

    def rows(start, size):
        return pl.ds(pl.multiple_of(start, 8), size)

    def cols(start, size):
        return pl.ds(pl.multiple_of(start, 128), size)

    barrier = pltpu.get_barrier_semaphore()
    partners = [dev(sib, x), dev(nxt, x), dev(prv, x)]
    for d in range(1, 4):
        partners += [dev(s, mod(x + d, 4)), dev(seq_of(z, mod(y + d, 4)), x), dev(seq_of(mod(z + d, 4), y), x)]
    for partner in partners:
        pl.semaphore_signal(barrier, inc=1, device_id=partner, device_id_type=MESH_ID)

    def load_w(p, _):
        for half in range(2):
            pltpu.make_async_copy(
                w_h.at[:, cols(half * 2048 + p * PW, PW)],
                wv.at[p, rows(x * 192, 192), pl.ds(half * PW, PW)],
                load_sem.at[p],
            ).start()
        return 0

    lax.fori_loop(0, PAIRS, load_w, 0)
    own_nb = pltpu.make_async_copy(nb_h.at[pl.ds(0, 768)], nbx.at[pl.ds(256, 768)], nb_sem)
    own_nb.start()
    pt_copy = pltpu.make_async_copy(pt_h, ptv, pt_sem)
    pt_copy.start()

    token_copies = [
        pltpu.make_async_copy(src, dst, tok_sem.at[n])
        for n, (src, dst) in enumerate(
            ((q_h, qv), (k_h, kv.at[0, pl.ds(256, 256)]), (v_h, kv.at[1, pl.ds(256, 256)]), (do_h, dov), (cq_h, cqv))
        )
    ]
    for copy in token_copies:
        copy.start()

    for g in range(3):
        cntv[g + 1] = jnp.full((8, 128), cnt_s[0, g], jnp.int32)
    cntsend[...] = jnp.full((8, 128), cnt_s[0, 3], jnp.int32)
    own3[...] = jnp.zeros(own3.shape, F32)

    pl.semaphore_wait(barrier, len(partners))

    def w_first(p):
        wait(wv.at[p, rows(x * 192, 192)], load_sem.at[p])
        piece = wv.at[p, rows(x * 192 + c * 96, 96)]
        for where in (xr, xl):
            remote(piece, piece, w_sem.at[0, p], w_sem.at[1, p], dev(s, where)).start()

    def w_second(p):
        wait(wv.at[p, pl.ds(0, 192)], w_sem.at[1, p])
        from_left = wv.at[p, rows(xl * 192 + c * 96, 48)]
        from_right = wv.at[p, rows(xr * 192 + c * 96 + 48, 48)]
        remote(from_left, from_left, w_sem.at[2, p], w_sem.at[3, p], dev(s, xr)).start()
        remote(from_right, from_right, w_sem.at[2, p], w_sem.at[3, p], dev(s, xl)).start()
        for shard in (xl, xr):
            piece = wv.at[p, rows(shard * 192 + c * 96, 96)]
            remote(piece, piece, w_sem.at[4, p], w_sem.at[5, p], dev(sib, x)).start()

    def w_third(p):
        wait(wv.at[p, pl.ds(0, 96)], w_sem.at[3, p])
        piece = wv.at[p, rows(xa * 192 + c * 96, 96)]
        remote(piece, piece, w_sem.at[4, p], w_sem.at[5, p], dev(sib, x)).start()

    def w_done(p):
        wait(wv.at[p, pl.ds(0, 288)], w_sem.at[5, p])

    w_first(0)
    halo = remote(nb_h.at[pl.ds(768, 256)], nbx.at[pl.ds(0, 256)], nbh_sem.at[0], nbh_sem.at[1], dev(nxt, x))
    halo.start()
    count_copy = remote(cntsend, cntv.at[0], cnt_sem.at[0], cnt_sem.at[1], dev(nxt, x))
    count_copy.start()

    def send_kv(p):
        span = cols(p * PW, PW)
        for n, src in enumerate((k_h, v_h)):
            remote(src.at[:, span], kv.at[n, pl.ds(0, 256), span], kvx_sem.at[0, p], kvx_sem.at[1, p], dev(nxt, x)).start()

    send_kv(0)
    w_first(1)
    send_kv(1)
    w_first(2)
    send_kv(2)

    key_at = lax.broadcasted_iota(jnp.int32, (384, 128), 0)
    query_at = lax.broadcasted_iota(jnp.int32, (384, 128), 1)
    for b in range(2):
        allowed = (key_at > query_at) & (key_at <= query_at + TOK)
        allowed = allowed & ((key_at + b * 128 >= TOK) | jnp.logical_not(first))
        bias[b] = jnp.where(allowed, 0.0, -1e30).astype(F32)

    pt_copy.wait()
    own_nb.wait()

    def reorder(n, _):
        t = n // 3
        g = mod(n, 3) + 1
        nbt[t, :, cols(g * 256, 256)] = dot(ptv[t], nbx[rows(g * 256, 256)], NT).astype(BF16)
        return 0

    lax.fori_loop(0, 9, reorder, 0)
    w_second(0)
    w_first(3)
    halo.wait_recv()

    def reorder_halo(t, _):
        nbt[t, :, pl.ds(0, 256)] = dot(ptv[t], nbx[pl.ds(0, 256)], NT).astype(BF16)
        return 0

    lax.fori_loop(0, 3, reorder_halo, 0)
    count_copy.wait_recv()
    w_third(0)
    w_second(1)
    for copy in token_copies:
        copy.wait()

    def softmax_grads(sc, dp):
        e = jnp.exp2(sc - jnp.max(sc, axis=0, keepdims=True))
        inv = 1.0 / jnp.sum(e, axis=0, keepdims=True)
        probs = e * inv
        delta = jnp.sum(e * dp, axis=0, keepdims=True) * inv
        return probs, probs * ((dp - delta) * SCALE)

    def self_pair(p):
        wait(kv.at[:, pl.ds(0, 256), cols(p * PW, PW)], kvx_sem.at[1, p])
        slot = p
        zero = jnp.zeros((128, 128), BF16)
        for h in range(2):
            lanes = pl.ds(h * HD, HD)
            at = cols(p * PW + h * HD, HD)
            qh = qv[:, at]
            doh = dov[:, at]
            kh = kv[0, :, at]
            vh = kv[1, :, at]
            sc = dot(kh, qh, NT)
            dp = dot(vh, doh, NT)
            parts = []
            for b in range(2):
                near = slice(b * 128, b * 128 + 384)
                here = slice(b * 128, b * 128 + 128)
                probs, ds = softmax_grads(sc[near, here] * (SCALE * LOG2E) + bias[b], dp[near, here])
                parts.append((probs.astype(BF16), ds.astype(BF16)))
            for b, (probs, ds) in enumerate(parts):
                near = slice(b * 128, b * 128 + 384)
                selfout[p, pl.ds(b * 128, 128), lanes] = dot(probs, vh[near], TN)
                stage[1, pl.ds(b * 128, 128), at] = dot(ds, kh[near], TN).astype(BF16)

            def joined(n):
                return jnp.concatenate(
                    [jnp.concatenate([parts[0][n], zero], 0), jnp.concatenate([zero, parts[1][n]], 0)], 1
                )

            dv = dot(joined(0), doh)
            dk = dot(joined(1), qh)
            kvsend[p, 0, :, lanes] = dk[:TOK].astype(BF16)
            kvsend[p, 1, :, lanes] = dv[:TOK].astype(BF16)
            kvown[slot, 0, :, lanes] = dk[TOK:]
            kvown[slot, 1, :, lanes] = dv[TOK:]
        remote(kvsend.at[p], kvret.at[p], ret_sem.at[0, p], ret_sem.at[1, p], dev(prv, x)).start()
        write_out(1, dq_o, p)

    def write_out(n, dst, p):
        span = cols(p * PW, PW)
        pltpu.make_async_copy(stage.at[n, :, span], dst.at[:, span], out_sem.at[n, p]).start()

    def returned(p):
        wait(kvret.at[p], ret_sem.at[1, p])
        slot = p
        for n, dst in enumerate((dk_o, dv_o)):
            stage[3 + n, :, cols(p * PW, PW)] = (kvown[slot, n] + kvret[p, n].astype(F32)).astype(BF16)
            write_out(3 + n, dst, p)

    def cross_pair(p):
        lane = lax.broadcasted_iota(jnp.int32, (GROUP, PW), 1)
        key_row = lax.broadcasted_iota(jnp.int32, (256, 128), 0)
        zero = jnp.zeros((GROUP, PW), BF16)
        span = cols(p * PW, PW)
        live = [jnp.where(first, 0.0, 1.0).astype(F32), None, None, None]

        def both(a):
            return jnp.concatenate([jnp.where(lane < HD, a, zero), jnp.where(lane >= HD, a, zero)], 0)

        def split(a):
            return jnp.concatenate([a[:GROUP, :HD], a[GROUP:, HD:]], 1)

        groups = range(4)
        toks = [pl.ds(g * GROUP, GROUP) for g in groups]
        proj = [dot(nbx[pl.ds(g * 256, 256)], wv[p]).astype(BF16) for g in groups]
        kp = [a[:, :PW] for a in proj]
        vp = [a[:, PW:] for a in proj]
        qb = [both(cqv[tok, span]) for tok in toks]
        dob = [both(dov[tok, span]) for tok in toks]
        sc = [dot(kp[g], qb[g], NT) for g in groups]
        dp = [dot(vp[g], dob[g], NT) for g in groups]
        low = []
        for g in groups:
            used = key_row < cntv[g, pl.ds(0, 1), :] * RLEN
            probs, ds = softmax_grads(jnp.where(used, sc[g] * (SCALE * LOG2E), -1e30), dp[g])
            if live[g] is not None:
                probs, ds = probs * live[g], ds * live[g]
            low.append((probs.astype(BF16), ds.astype(BF16)))
        for g, (probs, ds) in enumerate(low):
            dkv[pl.ds(g * 256, 256), pl.ds(0, PW)] = dot(ds, qb[g]).astype(BF16)
            dkv[pl.ds(g * 256, 256), pl.ds(PW, PW)] = dot(probs, dob[g]).astype(BF16)
        weight_grad(p)
        for g, (probs, ds) in enumerate(low):
            crossout[p, toks[g], :] = split(dot(probs, vp[g], TN))
            stage[2, toks[g], span] = split(dot(ds, kp[g], TN)).astype(BF16)
        write_out(2, dcq_o, p)

    def finish_out(p):
        span = cols(p * PW, PW)
        stage[0, :, span] = (selfout[p] + crossout[p]).astype(BF16)
        write_out(0, out_o, p)

    def kind(p, n):
        if n:
            return 1 + p // 4
        return mod(p, 4) // 2 * (1 - mod(p, 2)) * (2 - p // 4)

    def places(p, n):
        t = kind(p, n)
        a, b, e = (2 - t) // 2, mod(t, 2), t // 2
        return a * z + b * y + e * x, a * y + b * x + e * z, a * x + b * z + e * y

    def peer(p, n, order, d):
        t = kind(p, n)
        a, b, e = d * ((2 - t) // 2), d * mod(t, 2), d * (t // 2)
        dz, dy, dx = ((a, b, e), (e, a, b), (b, e, a))[order]
        return dev(seq_of(mod(z + dz, 4), mod(y + dy, 4)), mod(x + dx, 4))

    def weight_grad(p):
        slot = mod(p, 2)
        for n in range(2):
            u = 2 * p + n
            t = kind(p, n)
            grads = dkv[:, pl.ds(n * PW, PW)]
            csend[u] = dot(nbt[t, rows((1 - c) * 384, 384), :], grads).astype(BF16)
            remote(csend.at[u], crecv.at[u], rs_sem.at[0, u], rs_sem.at[1, u], dev(sib, x)).start()
        for n in range(2):
            u = 2 * p + n
            t = kind(p, n)
            grads = dkv[:, pl.ds(n * PW, PW)]
            own[slot, n] = dot(nbt[t, rows(c * 384, 384), :], grads)

    def rs_core(p, n):
        u = 2 * p + n
        slot = mod(p, 2)
        m1, _, _ = places(p, n)
        wait(crecv.at[u], rs_sem.at[1, u])
        for d in (2, 1, 3):
            span = rows(mod(m1 + d, 4) * 96, 96)
            s1send[u, d - 1] = (own[slot, n, span, :] + crecv[u, span, :].astype(F32)).astype(BF16)
            remote(s1send.at[u, d - 1], s1recv.at[u, d - 1], rs_sem.at[2, u], rs_sem.at[3, u], peer(p, n, 0, d)).start()
        span = rows(m1 * 96, 96)
        own1[p, n] = own[slot, n, span, :] + crecv[u, span, :].astype(F32)

    def rs_first(p, n):
        u = 2 * p + n
        slot = mod(p, 2)
        _, m2, _ = places(p, n)
        wait(s1recv.at[u], rs_sem.at[3, u])
        t1[...] = own1[p, n] + ((s1recv[u, 0].astype(F32) + s1recv[u, 1].astype(F32)) + s1recv[u, 2].astype(F32))
        for d in (2, 1, 3):
            piece = t1[rows(mod(m2 + d, 4) * 24, 24), :]
            s2send[u, d - 1] = jnp.concatenate([piece[:, :128], piece[:, 128:]], 0).astype(BF16)
            remote(s2send.at[u, d - 1], s2recv.at[u, d - 1], rs_sem.at[4, u], rs_sem.at[5, u], peer(p, n, 1, d)).start()
        own2[p, n] = t1[rows(m2 * 24, 24), :]

    def rs_second(p, n):
        u = 2 * p + n
        slot = mod(p, 2)
        _, _, m3 = places(p, n)
        wait(s2recv.at[u], rs_sem.at[5, u])
        got = [s2recv[u, d].astype(F32) for d in range(3)]
        got = (got[0] + got[1]) + got[2]
        total = own2[p, n] + jnp.concatenate([got[:24], got[24:]], 1)
        for a in range(4):
            piece = total[a * 6 : a * 6 + 6]
            own3[p, n, a, pl.ds(0, 6), :] = piece
            piece = jnp.concatenate([piece, jnp.zeros((2, PW), F32)], 0)
            s3send[u, a] = jnp.concatenate([piece[:, :128], piece[:, 128:]], 0).astype(BF16)
        for d in (2, 1, 3):
            remote(s3send.at[u, mod(m3 + d, 4)], s3recv.at[u, d - 1], rs_sem.at[6, u], rs_sem.at[7, u], peer(p, n, 2, d)).start()

    def rs_third(p, n):
        u = 2 * p + n
        _, _, m3 = places(p, n)
        wait(s3recv.at[u], rs_sem.at[7, u])
        got = [s3recv[u, d].astype(F32) for d in range(3)]
        got = (got[0] + got[1]) + got[2]
        dw_o[:, cols(n * 2048 + p * PW, PW)] = own3[p, n, m3] + jnp.concatenate([got[:8], got[8:]], 1)

    def step(i, _):
        @pl.when(i < PAIRS - 2)
        def _():
            w_second(i + 2)

        @pl.when(i < PAIRS - 3)
        def _():
            send_kv(i + 3)

        @pl.when(i < PAIRS - 4)
        def _():
            w_first(i + 4)

        @pl.when(i < PAIRS - 1)
        def _():
            self_pair(i)
            w_third(i + 1)

        for lag, stage_of in ((1, rs_core), (3, rs_first), (5, rs_second), (7, rs_third)):

            @pl.when((i >= lag) & (i < PAIRS + lag))
            def _(lag=lag, stage_of=stage_of):
                for n in range(2):
                    stage_of(i - lag, n)

        @pl.when(i < PAIRS)
        def _():
            w_done(i)
            cross_pair(i)

        @pl.when(i == PAIRS)
        def _():
            self_pair(PAIRS - 1)

        @pl.when(i >= PAIRS - 1)
        def _():
            finish_out(i - PAIRS + 1)
            returned(i - PAIRS + 1)

        return 0

    lax.fori_loop(0, PAIRS + 7, step, 0)

    halo.wait_send()
    count_copy.wait_send()

    def drain(p, _):
        wait(kv.at[:, pl.ds(0, 256), cols(p * PW, PW)], kvx_sem.at[0, p])
        wait(wv.at[p, pl.ds(0, 192)], w_sem.at[0, p])
        wait(wv.at[p, pl.ds(0, 96)], w_sem.at[2, p])
        wait(wv.at[p, pl.ds(0, 288)], w_sem.at[4, p])
        wait(kvsend.at[p], ret_sem.at[0, p])
        for n in range(5):
            wait(stage.at[n, :, cols(p * PW, PW)], out_sem.at[n, p])
        for n in range(2):
            u = 2 * p + n
            wait(csend.at[u], rs_sem.at[0, u])
            wait(s1send.at[u], rs_sem.at[2, u])
            wait(s2send.at[u], rs_sem.at[4, u])
            wait(s3recv.at[u], rs_sem.at[6, u])
        return 0

    lax.fori_loop(0, PAIRS, drain, 0)


def finish(*refs):
    ins, outs, slabs, tail, sem = refs[:6], refs[6:12], refs[12], refs[13], refs[14]
    parts = [(ins[5], tail, outs[5])]
    for n in range(5):
        for piece in range(4):
            span = pl.ds(piece * 64, 64)
            parts.append((ins[n].at[span], slabs.at[n, span], outs[n].at[span]))
    reads = [pltpu.make_async_copy(a, b, sem.at[0, n]) for n, (a, b, _) in enumerate(parts)]
    writes = [pltpu.make_async_copy(b, c, sem.at[1, n]) for n, (_, b, c) in enumerate(parts)]
    for copy in reads:
        copy.start()
    for read, write in zip(reads, writes):
        read.wait()
        write.start()
    for copy in writes:
        copy.wait()


def on_device(
    self_query, self_key, self_value, cross_query, neighbours, neighbour_count, kv_weight, out_grad
):
    any_spec = pl.BlockSpec(memory_space=pl.ANY)
    slab = jax.ShapeDtypeStruct((TOK, HEADS * HD), BF16)
    dma = pltpu.SemaphoreType.DMA
    subs = 2 * PAIRS
    scratch = [
        pltpu.VMEM((TOK, HEADS * HD), BF16),
        pltpu.VMEM((TOK, HEADS * HD), BF16),
        pltpu.VMEM((TOK, HEADS * HD), BF16),
        pltpu.VMEM((2, 2 * TOK, HEADS * HD), BF16),
        pltpu.VMEM((1024, ENC), BF16),
        pltpu.VMEM((3, ENC, ENC), BF16),
        pltpu.VMEM((3, ENC, 1024), BF16),
        pltpu.VMEM((PAIRS, ENC, 2 * PW), BF16),
        pltpu.VMEM((PAIRS, 2, TOK, PW), BF16),
        pltpu.VMEM((PAIRS, 2, TOK, PW), BF16),
        pltpu.VMEM((PAIRS, 2, TOK, PW), F32),
        pltpu.VMEM((5, TOK, HEADS * HD), BF16),
        pltpu.VMEM((2, 384, 128), F32),
        pltpu.VMEM((PAIRS, TOK, PW), F32),
        pltpu.VMEM((PAIRS, TOK, PW), F32),
        pltpu.VMEM((1024, 2 * PW), BF16),
        pltpu.VMEM((4, 8, 128), jnp.int32),
        pltpu.VMEM((8, 128), jnp.int32),
        pltpu.VMEM((2, 2, 384, PW), F32),
        pltpu.VMEM((subs, 384, PW), BF16),
        pltpu.VMEM((subs, 384, PW), BF16),
        pltpu.VMEM((PAIRS, 2, 96, PW), F32),
        pltpu.VMEM((96, PW), F32),
        pltpu.VMEM((subs, 3, 96, PW), BF16),
        pltpu.VMEM((subs, 3, 96, PW), BF16),
        pltpu.VMEM((PAIRS, 2, 24, PW), F32),
        pltpu.VMEM((subs, 3, 48, 128), BF16),
        pltpu.VMEM((subs, 3, 48, 128), BF16),
        pltpu.VMEM((PAIRS, 2, 4, 8, PW), F32),
        pltpu.VMEM((subs, 4, 16, 128), BF16),
        pltpu.VMEM((subs, 3, 16, 128), BF16),
        dma((PAIRS,)),
        dma(()),
        dma((5,)),
        dma(()),
        dma((2,)),
        dma((2,)),
        dma((2, PAIRS)),
        dma((6, PAIRS)),
        dma((2, PAIRS)),
        dma((5, PAIRS)),
        dma((8, subs)),
    ]
    out, dq, dk, dv, dcq, dw = pl.pallas_call(
        kernel,
        out_shape=[slab] * 5 + [jax.ShapeDtypeStruct((8, 2 * HEADS * HD), F32)],
        in_specs=[any_spec] * 5 + [pl.BlockSpec(memory_space=pltpu.SMEM)] + [any_spec] * 3,
        out_specs=[any_spec] * 5 + [pl.BlockSpec(memory_space=pltpu.VMEM)],
        scratch_shapes=scratch,
        compiler_params=pltpu.CompilerParams(
            collective_id=0, has_side_effects=True, vmem_limit_bytes=60 * 1024 * 1024
        ),
        cost_estimate=pl.CostEstimate(flops=20_000_000_000, bytes_accessed=20_000_000, transcendentals=3_000_000),
    )(
        self_query[0],
        self_key[0],
        self_value[0],
        cross_query[0],
        neighbours.reshape(1024, ENC),
        neighbour_count,
        kv_weight,
        out_grad[0],
        jnp.asarray(row_orders()),
    )
    out, dq, dk, dv, dcq, dw = pl.pallas_call(
        finish,
        out_shape=[slab] * 5 + [jax.ShapeDtypeStruct((8, 2 * HEADS * HD), F32)],
        in_specs=[any_spec] * 6,
        out_specs=[any_spec] * 6,
        scratch_shapes=[
            pltpu.VMEM((5, TOK, HEADS * HD), BF16),
            pltpu.VMEM((8, 2 * HEADS * HD), F32),
            dma((2, 21)),
        ],
        cost_estimate=pl.CostEstimate(flops=0, bytes_accessed=10_000_000, transcendentals=0),
    )(out, dq, dk, dv, dcq, dw)
    return out[None], dq[None], dk[None], dv[None], dcq[None], dw[:6]


def solution(mesh):
    in_specs = (
        P("fsdp", "seq", None),
        P("fsdp", "seq", None),
        P("fsdp", "seq", None),
        P("fsdp", "seq", None),
        P("fsdp", "seq", None, None),
        P("fsdp", "seq"),
        P("fsdp", None),
        P("fsdp", "seq", None),
    )
    out_specs = (
        P("fsdp", "seq", None),
        P("fsdp", "seq", None),
        P("fsdp", "seq", None),
        P("fsdp", "seq", None),
        P("fsdp", "seq", None),
        P(("seq", "fsdp"), None),
    )
    return jax.shard_map(
        on_device, mesh=mesh, in_specs=in_specs, out_specs=out_specs, check_vma=False
    )
```
